32 devices in a mesh: wide: 16 (over z, y, core), narrow: 2 (over x).
Axes of the slice: x: 2, y: 2, z: 4, core: 2. Of those that a mesh axis runs over, the one named last changes fastest.
Arguments:
- tensor: bfloat16 [4, 1024, 2048], P('narrow', 'wide'), may hold values from -6 to 6
- factor_a: bfloat16 [32, 1024], P(None, 'wide'), may hold values from -0.4375 to 0.4375
- factor_b: bfloat16 [32, 2048], P(None, 'wide'), may hold values from -0.3125 to 0.3125
- factor_c: bfloat16 [32, 4], P(None, 'narrow'), may hold values from -6 to 6
Outputs:
- step_a: float32 [32, 1024], P(None, 'wide')
- step_b: float32 [32, 2048], P(None, 'wide')
- step_c: float32 [32, 4], P(None, 'narrow')
The draws below stay inside these ranges and needn't reach their ends.
All inputs are finite; a program needn't handle non-finite values.
Results may differ from the reference program's by a relative error of at most 0.0029.
Values may be sent and summed in bfloat16 or wider, within the bound.
A program may use at most 64 MiB of HBM per device.

```python
import jax
import jax.numpy as jnp
from jax import lax

R = 32
ITERS = 2
I = 1024
J = 2048
K = 4


def spiked(array, own_key, source, target, blocks, factor):
    def block_of(position):
        return (jnp.arange(array.shape[position]) // (array.shape[position] // blocks)).reshape((-1,) + (1,) * (array.ndim - 1 - position))

    one_side = jax.random.permutation(own_key, blocks)[block_of(target)]
    second = (block_of(target) + blocks // 2) % blocks
    return jnp.where((block_of(source) == one_side) | (block_of(source) == second), factor * array, array)


def block_levels(key, dims, pieces, low, top_value):
    def one(axis_at, blocks):
        steps = jax.random.uniform(jax.random.fold_in(jax.random.fold_in(key, 6), axis_at), (blocks,), jnp.float32, low / len(pieces), top_value / len(pieces))
        return jnp.repeat(jnp.exp(steps), dims[axis_at] // blocks).reshape((-1,) + (1,) * (len(dims) - axis_at - 1))

    factor_of = one(*pieces[0])
    for cut in pieces[1:]:
        factor_of = factor_of * one(*cut)
    return factor_of


def gaussian(key, extent, deviation, reach, cuts=(), held_as=jnp.bfloat16):
    array = jax.random.normal(key, extent, jnp.float32) * deviation
    if len(cuts) > 0:
        array = block_levels(key, extent, cuts, -0.22, 0.18) * array
    return jnp.clip(array, min=-reach, max=reach).astype(held_as)


def heavy_noise(stream_key, extent, spread, most, cuts, heavy, kind=jnp.bfloat16):
    result = spread * jax.random.normal(stream_key, extent, jnp.float32)
    if cuts:
        result = result * block_levels(stream_key, extent, cuts, -0.22, 0.18)
    return jnp.clip(spiked(result, jax.random.fold_in(stream_key, 3), *heavy), -most, most).astype(kind)


def setup_inputs(seed: int = 0) -> dict:
    arg_keys = jax.random.split(jax.random.key(seed), 5)
    tensor = heavy_noise(arg_keys[0], (K, I, J), 1.0, 6.0, ((0, 2), (1, 16)), (1, 2, 16, 2.0))
    factor_a = gaussian(arg_keys[1], (R, I), (I // 6) ** -0.5, 0.4375, ((1, 16),))
    factor_b = gaussian(arg_keys[2], (R, J), (J // 6) ** -0.5, 0.3125, ((1, 16),))
    factor_c = gaussian(arg_keys[3], (R, K), (max(1, K // 6)) ** -0.5, 6.0, ((1, 2),))
    return dict(tensor=tensor, factor_a=factor_a, factor_b=factor_b, factor_c=factor_c)


damping = 1.0
highest = lax.Precision.HIGHEST


def matmul(left, right):
    return jnp.dot(left, right, precision=highest)


def outer_rows(left, right):
    return lax.dot_general(left, right, (((1,), (1,)), ((), ())), precision=highest)


def gram_product(factors, grams, directions):
    float_a, float_b, float_c = factors
    gram_a, gram_b, gram_c = grams
    dir_a, dir_b, dir_c = directions
    cross_a = outer_rows(float_a, dir_a)
    cross_b = outer_rows(float_b, dir_b)
    cross_c = outer_rows(float_c, dir_c)
    image_a = matmul(gram_b * gram_c, dir_a) + matmul(cross_b * gram_c + gram_b * cross_c, float_a) + damping * dir_a
    image_b = matmul(gram_a * gram_c, dir_b) + matmul(cross_a * gram_c + gram_a * cross_c, float_b) + damping * dir_b
    image_c = matmul(gram_a * gram_b, dir_c) + matmul(cross_a * gram_b + gram_a * cross_b, float_c) + damping * dir_c
    return image_a, image_b, image_c


def inner_all(left, right):
    return jnp.sum(left[0] * right[0]) + jnp.sum(left[1] * right[1]) + jnp.sum(left[2] * right[2])


def reference(tensor, factor_a, factor_b, factor_c):
    flattened = tensor.reshape(K * I, J)
    contracted = lax.dot_general(factor_b, flattened, (((1,), (1,)), ((), ())), preferred_element_type=jnp.float32).reshape(R, K, I)
    float_a = factor_a.astype(jnp.float32)
    float_b = factor_b.astype(jnp.float32)
    float_c = factor_c.astype(jnp.float32)
    mttkrp_a = jnp.einsum("rk,rki->ri", float_c, contracted, precision=highest)
    mttkrp_c = jnp.einsum("ri,rki->rk", float_a, contracted, precision=highest)
    khatri = (float_c[:, :, None] * float_a[:, None, :]).reshape(R, K * I).astype(jnp.bfloat16)
    mttkrp_b = jnp.dot(khatri, flattened, preferred_element_type=jnp.float32)
    gram_a = jnp.dot(factor_a, factor_a.T, preferred_element_type=jnp.float32)
    gram_b = jnp.dot(factor_b, factor_b.T, preferred_element_type=jnp.float32)
    gram_c = jnp.dot(factor_c, factor_c.T, preferred_element_type=jnp.float32)
    grad_a = matmul(gram_b * gram_c, float_a) - mttkrp_a
    grad_b = matmul(gram_a * gram_c, float_b) - mttkrp_b
    grad_c = matmul(gram_a * gram_b, float_c) - mttkrp_c
    factors = (float_a, float_b, float_c)
    grams = (gram_a, gram_b, gram_c)
    resid = (-grad_a, -grad_b, -grad_c)
    direction = resid
    steps = (jnp.zeros_like(grad_a), jnp.zeros_like(grad_b), jnp.zeros_like(grad_c))
    norm_now = inner_all(resid, resid)
    for iteration in range(ITERS):
        image = gram_product(factors, grams, direction)
        step_size = norm_now / inner_all(direction, image)
        steps = tuple(old + step_size * move for old, move in zip(steps, direction))
        if iteration + 1 < ITERS:
            resid = tuple(old - step_size * move for old, move in zip(resid, image))
            norm_next = inner_all(resid, resid)
            momentum = norm_next / norm_now
            direction = tuple(now + momentum * old for now, old in zip(resid, direction))
            norm_now = norm_next
    return steps[0], steps[1], steps[2]
```

```python
import functools

import jax
import jax.numpy as jnp
from jax import lax
from jax.experimental import pallas as pl
from jax.experimental.pallas import tpu as pltpu
from jax.sharding import PartitionSpec as P

MESH = pl.DeviceIdType.MESH
highest = lax.Precision.HIGHEST
damping = 1.0


def mm(left, right):
    return jnp.dot(left, right, precision=highest, preferred_element_type=jnp.float32)


def nt(left, right, precision=highest):
    return lax.dot_general(
        left, right, (((1,), (1,)), ((), ())), precision=precision, preferred_element_type=jnp.float32
    )


def total(value):
    return jnp.sum(jnp.sum(value, axis=0, keepdims=True), axis=1, keepdims=True)


def kernel(
    wide, narrow, k_local, t_hbm, a_ref, b_ref, c_ref, out_a, out_b, out_c,
    t_ref, b_all, pb_send, pb_all, q_send, q_all, w_send, w_all, m_send, m_all, s_send, s_all,
    t_sem, b_sem, pb_sem, q_sem, w_sem, m_sem, s_sem,
):
    me = lax.axis_index("wide")
    row = lax.axis_index("narrow")
    core = lax.rem(me, 2)
    chip = me // 2
    chips = wide // 2
    quad = 2 * narrow
    rank, i_local = a_ref.shape
    j_local = b_ref.shape[1]
    k_whole = narrow * k_local

    load = pltpu.make_async_copy(t_hbm, t_ref, t_sem)
    load.start()

    def wide_peer(step):
        return lax.rem(me + step, wide)

    def quad_peer(step):
        mine = row * 2 + core
        other = lax.rem(mine + step, quad)
        return other // 2, chip * 2 + lax.rem(other, 2)

    barrier = pltpu.get_barrier_semaphore()

    def greet(step, carry):
        pl.semaphore_signal(barrier, inc=1, device_id=(wide_peer(step), row), device_id_type=MESH)
        return carry

    lax.fori_loop(1, wide, greet, 0)

    def greet_row(step, carry):
        there = lax.rem(row + step, narrow)
        for side in range(2):
            pl.semaphore_signal(
                barrier, inc=1, device_id=(chip * 2 + side, there), device_id_type=MESH
            )
        return carry

    lax.fori_loop(1, narrow, greet_row, 0)
    pl.semaphore_wait(barrier, (wide - 1) + 2 * (narrow - 1))

    def send(src, dst, sems, device):
        pltpu.make_async_remote_copy(
            src_ref=src, dst_ref=dst, send_sem=sems.at[0], recv_sem=sems.at[1],
            device_id=device, device_id_type=MESH,
        ).start()

    def settle(buffer, count, sem):
        if count > 0:
            part = buffer.at[pl.ds(0, count)]
            pltpu.make_async_copy(part, part, sem).wait()

    def send_b(step, carry):
        send(b_ref, b_all.at[me], b_sem, (wide_peer(step), row))
        return carry

    lax.fori_loop(1, wide, send_b, 0)
    b_all[me] = b_ref[...]

    fa = a_ref[...].astype(jnp.float32)
    fc = c_ref[...].astype(jnp.float32)
    a_rep = jnp.concatenate([fa] * k_local, axis=1)
    c_rep = jnp.concatenate(
        [jnp.broadcast_to(fc[:, k : k + 1], (rank, i_local)) for k in range(k_local)], axis=1
    )
    khatri = (a_rep * c_rep).astype(jnp.bfloat16)
    load.wait()
    partial_b = jnp.dot(khatri, t_ref[...], preferred_element_type=jnp.float32).astype(jnp.bfloat16)
    for w in range(wide):
        pb_send[w] = partial_b[:, w * j_local : (w + 1) * j_local]

    def send_pb(step, carry):
        there = wide_peer(step)
        send(pb_send.at[there], pb_all.at[me], pb_sem, (there, row))
        return carry

    lax.fori_loop(1, wide, send_pb, 0)
    pb_all[me] = pb_send[me]
    gram_a_own = nt(fa, fa)

    settle(b_all, wide - 1, b_sem.at[1])
    factor_b = jnp.concatenate([b_all[w] for w in range(wide)], axis=1)
    contracted = nt(factor_b, t_ref[...], None)
    weighted = c_rep * contracted
    part_a = weighted[:, :i_local]
    for k in range(1, k_local):
        part_a = part_a + weighted[:, k * i_local : (k + 1) * i_local]
    pair_a = nt(a_rep, weighted)
    pair_b = nt(contracted, khatri.astype(jnp.float32))
    lane = lax.broadcasted_iota(jnp.int32, (rank, 128), 1)
    used = 3 * rank
    share = jnp.where(row == 0, 1.0, 0.0)
    small = jnp.concatenate(
        [pair_a, pair_b, gram_a_own * share, jnp.zeros((rank, 128 - used), jnp.float32)], axis=1
    )
    first = jnp.where(me == 0, 1.0, 0.0)
    product = a_rep * contracted
    for k in range(k_local):
        at = used + row * k_local + k
        column = jnp.sum(product[:, k * i_local : (k + 1) * i_local], axis=1, keepdims=True)
        small = small + jnp.where(lane == at, column, 0.0)
        small = small + jnp.where(lane == at + k_whole, fc[:, k : k + 1] * first, 0.0)
    q_send[...] = small
    q_all[row * 2 + core] = small

    def send_q(step, carry):
        there_row, there = quad_peer(step)
        send(q_send, q_all.at[row * 2 + core], q_sem, (there, there_row))
        return carry

    lax.fori_loop(1, quad, send_q, 0)

    settle(pb_all, wide - 1, pb_sem.at[1])
    part_b = jnp.sum(pb_all[...].astype(jnp.float32), axis=0)
    m_send[0] = part_b
    m_send[1, :, :i_local] = part_a
    m_all[row] = m_send[...]

    def send_m(step, carry):
        there = lax.rem(row + step, narrow)
        send(m_send, m_all.at[row], m_sem, (me, there))
        return carry

    gram_b = nt(factor_b, factor_b, None)
    settle(q_all, quad - 1, q_sem.at[1])
    small = jnp.sum(q_all[...], axis=0)
    w_send[...] = small
    w_all[chip] = small

    def send_w(step, carry):
        there = lax.rem(chip + step, chips)
        send(w_send, w_all.at[chip], w_sem, (there * 2 + core, row))
        return carry

    lax.fori_loop(1, chips, send_w, 0)
    lax.fori_loop(1, narrow, send_m, 0)
    settle(w_all, chips - 1, w_sem.at[1])
    small = jnp.sum(w_all[...], axis=0)

    pair_a = small[:, :rank]
    pair_b = small[:, rank : 2 * rank]
    gram_a = small[:, 2 * rank : used]
    mttkrp_c = small[:, used : used + k_whole]
    whole_c = small[:, used + k_whole : used + 2 * k_whole]
    fb = b_ref[...].astype(jnp.float32)

    gram_c = nt(whole_c, whole_c)
    had_a = gram_b * gram_c
    had_b = gram_a * gram_c
    had_c = gram_a * gram_b
    grad_c = mttkrp_c - mm(had_c, whole_c)
    cross_a = pair_a - mm(gram_a, had_a)
    cross_b = pair_b - mm(gram_b, had_b)
    cross_c = nt(whole_c, grad_c)
    mixed_a = cross_b * gram_c + gram_b * cross_c
    mixed_b = cross_a * gram_c + gram_a * cross_c
    mixed_c = cross_a * gram_b + gram_a * cross_b

    settle(m_all, narrow - 1, m_sem.at[1])
    summed = jnp.sum(m_all[...], axis=0)
    grad_a = summed[1][:, :i_local] - mm(had_a, fa)
    grad_b = summed[0] - mm(had_b, fb)

    had_grad_a = mm(had_a, grad_a)
    had_grad_b = mm(had_b, grad_b)
    had_grad_c = mm(had_c, grad_c)
    image_a = had_grad_a + mm(mixed_a, fa) + damping * grad_a
    image_b = had_grad_b + mm(mixed_b, fb) + damping * grad_b
    image_c = had_grad_c + mm(mixed_c, whole_c) + damping * grad_c
    sums = (
        total(grad_a * grad_a) + total(grad_b * grad_b),
        total(grad_a * had_grad_a) + total(grad_b * had_grad_b),
        total(image_a * image_a) + total(image_b * image_b),
        total(image_a * mm(had_a, image_a)) + total(image_b * mm(had_b, image_b)),
    )
    line = lax.broadcasted_iota(jnp.int32, (8, 128), 0)
    tile = jnp.zeros((8, 128), jnp.float32)
    for at, value in enumerate(sums):
        tile = jnp.where(line == at, value, tile)
    s_send[...] = tile
    s_all[me] = tile

    def send_s(step, carry):
        send(s_send, s_all.at[me], s_sem, (wide_peer(step), row))
        return carry

    lax.fori_loop(1, wide, send_s, 0)

    next_a = mm(cross_a, had_a) + damping * cross_a + nt(gram_a, mixed_a)
    next_b = mm(cross_b, had_b) + damping * cross_b + nt(gram_b, mixed_b)
    next_c = nt(whole_c, image_c)
    later_a = next_b * gram_c + gram_b * next_c
    later_b = next_a * gram_c + gram_a * next_c
    later_c = next_a * gram_b + gram_a * next_b
    known_gg = total(grad_c * grad_c)
    known_gh = total(grad_c * had_grad_c) + total(
        mixed_a * cross_a.T + mixed_b * cross_b.T + mixed_c * cross_c.T
    )
    known_qq = total(image_c * image_c)
    known_qh = total(image_c * mm(had_c, image_c)) + total(
        later_a * next_a.T + later_b * next_b.T + later_c * next_c.T
    )

    settle(s_all, wide - 1, s_sem.at[1])
    tile = jnp.sum(s_all[...], axis=0)
    norm_0 = tile[0:1, 0:1] + known_gg
    curve_0 = tile[1:2, 0:1] + known_gh + damping * norm_0
    image_2 = tile[2:3, 0:1] + known_qq
    image_3 = tile[3:4, 0:1] + known_qh + damping * image_2

    alpha_0 = norm_0 / curve_0
    norm_1 = norm_0 - 2.0 * alpha_0 * curve_0 + alpha_0 * alpha_0 * image_2
    beta = norm_1 / norm_0
    gain = 1.0 + beta
    curve_1 = gain * gain * curve_0 - 2.0 * gain * alpha_0 * image_2 + alpha_0 * alpha_0 * image_3
    alpha_1 = norm_1 / curve_1
    on_grad = alpha_0 + alpha_1 * gain
    on_image = -alpha_1 * alpha_0
    out_a[...] = on_grad * grad_a + on_image * image_a
    out_b[...] = on_grad * grad_b + on_image * image_b
    step_c = on_grad * grad_c + on_image * image_c
    lane_c = lax.broadcasted_iota(jnp.int32, (rank, k_whole), 1)
    for k in range(k_local):
        picked = jnp.where(lane_c == row * k_local + k, step_c, 0.0)
        out_c[:, k : k + 1] = jnp.sum(picked, axis=1, keepdims=True)

    settle(b_all, wide - 1, b_sem.at[0])
    settle(pb_all, wide - 1, pb_sem.at[0])
    settle(q_all, quad - 1, q_sem.at[0])
    settle(w_all, chips - 1, w_sem.at[0])
    settle(m_all, narrow - 1, m_sem.at[0])
    settle(s_all, wide - 1, s_sem.at[0])


def on_device(wide, narrow, tensor, factor_a, factor_b, factor_c):
    k_local, i_local, j_whole = tensor.shape
    rank, j_local = factor_b.shape
    flattened = tensor.reshape(k_local * i_local, j_whole)
    vmem = pl.BlockSpec(memory_space=pltpu.VMEM)
    pair = pltpu.SemaphoreType.DMA((2,))
    f32, bf16 = jnp.float32, jnp.bfloat16
    return pl.pallas_call(
        functools.partial(kernel, wide, narrow, k_local),
        out_shape=(
            jax.ShapeDtypeStruct((rank, i_local), f32),
            jax.ShapeDtypeStruct((rank, j_local), f32),
            jax.ShapeDtypeStruct((rank, k_local), f32),
        ),
        in_specs=[pl.BlockSpec(memory_space=pl.ANY), vmem, vmem, vmem],
        out_specs=(vmem, vmem, vmem),
        scratch_shapes=[
            pltpu.VMEM((k_local * i_local, j_whole), bf16),
            pltpu.VMEM((wide, rank, j_local), bf16),
            pltpu.VMEM((wide, rank, j_local), bf16),
            pltpu.VMEM((wide, rank, j_local), bf16),
            pltpu.VMEM((rank, 128), f32),
            pltpu.VMEM((2 * narrow, rank, 128), f32),
            pltpu.VMEM((rank, 128), f32),
            pltpu.VMEM((wide // 2, rank, 128), f32),
            pltpu.VMEM((2, rank, 128), f32),
            pltpu.VMEM((narrow, 2, rank, 128), f32),
            pltpu.VMEM((8, 128), f32),
            pltpu.VMEM((wide, 8, 128), f32),
            pltpu.SemaphoreType.DMA,
            pair, pair, pair, pair, pair, pair,
        ],
        compiler_params=pltpu.CompilerParams(
            collective_id=0, has_side_effects=True, vmem_limit_bytes=48 * 1024 * 1024
        ),
    )(flattened, factor_a, factor_b, factor_c)


def solution(mesh):
    placed = (P("narrow", "wide", None), P(None, "wide"), P(None, "wide"), P(None, "narrow"))
    return jax.shard_map(
        functools.partial(on_device, mesh.shape["wide"], mesh.shape["narrow"]),
        mesh=mesh,
        in_specs=placed,
        out_specs=(P(None, "wide"), P(None, "wide"), P(None, "narrow")),
        check_vma=False,
    )
```

```python
import functools

import jax
import jax.numpy as jnp
from jax import lax
from jax.experimental import pallas as pl
from jax.experimental.pallas import tpu as pltpu
from jax.sharding import PartitionSpec as P

MESH = pl.DeviceIdType.MESH
highest = lax.Precision.HIGHEST
damping = 1.0


def mm(left, right):
    return jnp.dot(left, right, precision=highest, preferred_element_type=jnp.float32)


def nt(left, right, precision=highest):
    return lax.dot_general(
        left, right, (((1,), (1,)), ((), ())), precision=precision, preferred_element_type=jnp.float32
    )


def total(value):
    return jnp.sum(jnp.sum(value, axis=0, keepdims=True), axis=1, keepdims=True)


def kernel(
    wide, narrow, k_local, t_hbm, a_hbm, b_hbm, c_hbm, out_a, out_b, out_c,
    t_ref, a_ref, b_ref, c_ref, b_all, pb_send, pb_all, p_send, p_all, g_all, m_send, m_all, s_all,
    load_sem, b_sem, pb_sem, p_sem, g_sem, m_sem, s_sem,
):
    me = lax.axis_index("wide")
    row = lax.axis_index("narrow")
    devices = wide * narrow
    own = row * wide + me
    owners, rows = p_send.shape[0], p_send.shape[1]
    rank, i_local = a_ref.shape
    j_local = b_ref.shape[1]
    k_whole = narrow * k_local

    loads = [
        pltpu.make_async_copy(src, dst, load_sem.at[at])
        for at, (src, dst) in enumerate(
            ((b_hbm, b_ref), (c_hbm, c_ref), (a_hbm, a_ref), (t_hbm, t_ref))
        )
    ]
    for load in loads:
        load.start()

    def wide_peer(step):
        return lax.rem(me + step, wide)

    def device_of(position):
        return lax.rem(position, wide), position // wide

    barrier = pltpu.get_barrier_semaphore()

    def greet(step, carry):
        pl.semaphore_signal(
            barrier, inc=1, device_id=device_of(lax.rem(own + step, devices)), device_id_type=MESH
        )
        return carry

    lax.fori_loop(1, devices, greet, 0)
    for load in loads[:3]:
        load.wait()
    b_all[me] = b_ref[...]
    fa = a_ref[...].astype(jnp.float32)
    eye = jnp.where(
        lax.broadcasted_iota(jnp.int32, (rank, rank), 0)
        == lax.broadcasted_iota(jnp.int32, (rank, rank), 1),
        1.0,
        0.0,
    )
    fc = nt(eye.astype(jnp.bfloat16), c_ref[...], None)
    a_rep = jnp.concatenate([fa] * k_local, axis=1)
    c_rep = jnp.concatenate(
        [jnp.broadcast_to(fc[:, k : k + 1], (rank, i_local)) for k in range(k_local)], axis=1
    )
    khatri = (a_rep * c_rep).astype(jnp.bfloat16)
    gram_a_own = nt(a_ref[...], a_ref[...], None)
    pl.semaphore_wait(barrier, devices - 1)

    def send(src, dst, sems, device):
        pltpu.make_async_remote_copy(
            src_ref=src, dst_ref=dst, send_sem=sems.at[0], recv_sem=sems.at[1],
            device_id=device, device_id_type=MESH,
        ).start()

    def settle(buffer, count, sem):
        if count > 0:
            part = buffer.at[pl.ds(0, count)]
            pltpu.make_async_copy(part, part, sem).wait()

    def send_b(step, carry):
        send(b_ref, b_all.at[me], b_sem, (wide_peer(step), row))
        return carry

    lax.fori_loop(1, wide, send_b, 0)

    loads[3].wait()
    partial_b = jnp.dot(khatri, t_ref[...], preferred_element_type=jnp.float32).astype(jnp.bfloat16)
    for w in range(wide):
        pb_send[w] = partial_b[:, w * j_local : (w + 1) * j_local]

    def send_pb(step, carry):
        there = wide_peer(step)
        send(pb_send.at[there], pb_all.at[me], pb_sem, (there, row))
        return carry

    lax.fori_loop(1, wide, send_pb, 0)
    pb_all[me] = pb_send[me]

    settle(b_all, wide - 1, b_sem.at[1])
    factor_b = jnp.concatenate([b_all[w] for w in range(wide)], axis=1)
    contracted = nt(factor_b, t_ref[...], None)
    weighted = c_rep * contracted
    part_a = weighted[:, :i_local]
    for k in range(1, k_local):
        part_a = part_a + weighted[:, k * i_local : (k + 1) * i_local]
    pair_a = nt(a_rep, weighted)
    pair_b = nt(contracted, khatri.astype(jnp.float32))
    lane = lax.broadcasted_iota(jnp.int32, (rank, 128), 1)
    used = 3 * rank
    share = jnp.where(row == 0, 1.0, 0.0)
    small = jnp.concatenate(
        [pair_a, pair_b, gram_a_own * share, jnp.zeros((rank, 128 - used), jnp.float32)], axis=1
    )
    first = jnp.where(me == 0, 1.0, 0.0)
    product = a_rep * contracted
    for k in range(k_local):
        at = used + row * k_local + k
        column = jnp.sum(product[:, k * i_local : (k + 1) * i_local], axis=1, keepdims=True)
        small = small + jnp.where(lane == at, column, 0.0)
        small = small + jnp.where(lane == at + k_whole, fc[:, k : k + 1] * first, 0.0)
    p_send[...] = small.reshape(owners, rows, 128)

    def send_p(step, carry):
        owner = lax.rem(own + step, owners)

        def go():
            send(p_send.at[owner], p_all.at[own], p_sem, device_of(owner))

        if owners == devices:
            go()
        else:
            pl.when(owner != own)(go)
        return carry

    lax.fori_loop(1 if owners == devices else 0, owners, send_p, 0)
    gram_b = nt(factor_b, factor_b, None)

    def give():
        p_all[own] = p_send[own]
        settle(p_all, devices - 1, p_sem.at[1])
        g_all[own] = jnp.sum(p_all[...], axis=0)

        def send_g(step, carry):
            there = lax.rem(own + step, devices)
            send(g_all.at[own], g_all.at[own], g_sem, device_of(there))
            return carry

        lax.fori_loop(1, devices, send_g, 0)

    def taken():
        settle(g_all, owners - 1, g_sem.at[1])
        settle(p_all, owners - 1, p_sem.at[0])

    def taken_whole():
        settle(g_all, owners, g_sem.at[1])
        settle(p_all, owners, p_sem.at[0])

    if owners == devices:
        give()
    else:
        pl.when(own < owners)(give)

    settle(pb_all, wide - 1, pb_sem.at[1])
    part_b = jnp.sum(pb_all[...].astype(jnp.float32), axis=0)
    m_send[0] = part_b
    m_send[1, :, :i_local] = part_a
    m_all[row] = m_send[...]

    def send_m(step, carry):
        there = lax.rem(row + step, narrow)
        send(m_send, m_all.at[row], m_sem, (me, there))
        return carry

    lax.fori_loop(1, narrow, send_m, 0)
    if owners == devices:
        taken()
    else:
        pl.when(own < owners)(taken)
        pl.when(own >= owners)(taken_whole)
    small = g_all[...].reshape(rank, 128)

    pair_a = small[:, :rank]
    pair_b = small[:, rank : 2 * rank]
    gram_a = small[:, 2 * rank : used]
    mttkrp_c = small[:, used : used + k_whole]
    whole_c = small[:, used + k_whole : used + 2 * k_whole]
    fb = b_ref[...].astype(jnp.float32)

    gram_c = nt(whole_c, whole_c)
    had_a = gram_b * gram_c
    had_b = gram_a * gram_c
    had_c = gram_a * gram_b
    grad_c = mttkrp_c - mm(had_c, whole_c)
    cross_a = pair_a - mm(gram_a, had_a)
    cross_b = pair_b - mm(gram_b, had_b)
    cross_c = nt(whole_c, grad_c)
    mixed_a = cross_b * gram_c + gram_b * cross_c
    mixed_b = cross_a * gram_c + gram_a * cross_c
    mixed_c = cross_a * gram_b + gram_a * cross_b

    settle(m_all, narrow - 1, m_sem.at[1])
    summed = jnp.sum(m_all[...], axis=0)
    grad_a = summed[1][:, :i_local] - mm(had_a, fa)
    grad_b = summed[0] - mm(had_b, fb)

    had_grad_a = mm(had_a, grad_a)
    had_grad_b = mm(had_b, grad_b)
    had_grad_c = mm(had_c, grad_c)
    image_a = had_grad_a + mm(mixed_a, fa) + damping * grad_a
    image_b = had_grad_b + mm(mixed_b, fb) + damping * grad_b
    image_c = had_grad_c + mm(mixed_c, whole_c) + damping * grad_c
    sums = (
        total(grad_a * grad_a) + total(grad_b * grad_b),
        total(grad_a * had_grad_a) + total(grad_b * had_grad_b),
        total(image_a * image_a) + total(image_b * image_b),
        total(image_a * mm(had_a, image_a)) + total(image_b * mm(had_b, image_b)),
    )
    place = lax.broadcasted_iota(jnp.int32, (1, 128), 1)
    tile = jnp.zeros((1, 128), jnp.float32)
    for at, value in enumerate(sums):
        tile = jnp.where(place == at, value, tile)
    s_all[me] = tile

    def send_s(step, carry):
        send(s_all.at[me], s_all.at[me], s_sem, (wide_peer(step), row))
        return carry

    lax.fori_loop(1, wide, send_s, 0)

    next_a = mm(cross_a, had_a) + damping * cross_a + nt(gram_a, mixed_a)
    next_b = mm(cross_b, had_b) + damping * cross_b + nt(gram_b, mixed_b)
    next_c = nt(whole_c, image_c)
    later_a = next_b * gram_c + gram_b * next_c
    later_b = next_a * gram_c + gram_a * next_c
    later_c = next_a * gram_b + gram_a * next_b
    known_gg = total(grad_c * grad_c)
    known_gh = total(grad_c * had_grad_c) + total(
        mixed_a * cross_a.T + mixed_b * cross_b.T + mixed_c * cross_c.T
    )
    known_qq = total(image_c * image_c)
    known_qh = total(image_c * mm(had_c, image_c)) + total(
        later_a * next_a.T + later_b * next_b.T + later_c * next_c.T
    )

    settle(s_all, wide - 1, s_sem.at[1])
    tile = jnp.sum(s_all[...], axis=0)
    norm_0 = tile[:, 0:1] + known_gg
    curve_0 = tile[:, 1:2] + known_gh + damping * norm_0
    image_2 = tile[:, 2:3] + known_qq
    image_3 = tile[:, 3:4] + known_qh + damping * image_2

    alpha_0 = norm_0 / curve_0
    norm_1 = norm_0 - 2.0 * alpha_0 * curve_0 + alpha_0 * alpha_0 * image_2
    beta = norm_1 / norm_0
    gain = 1.0 + beta
    curve_1 = gain * gain * curve_0 - 2.0 * gain * alpha_0 * image_2 + alpha_0 * alpha_0 * image_3
    alpha_1 = norm_1 / curve_1
    on_grad = alpha_0 + alpha_1 * gain
    on_image = -alpha_1 * alpha_0
    out_a[...] = on_grad * grad_a + on_image * image_a
    out_b[...] = on_grad * grad_b + on_image * image_b
    step_c = on_grad * grad_c + on_image * image_c
    chosen = jnp.where(
        lax.broadcasted_iota(jnp.int32, (k_local, k_whole), 1)
        == lax.broadcasted_iota(jnp.int32, (k_local, k_whole), 0) + row * k_local,
        1.0,
        0.0,
    )
    out_c[...] = nt(chosen, step_c)

    settle(b_all, wide - 1, b_sem.at[0])
    settle(pb_all, wide - 1, pb_sem.at[0])
    settle(m_all, narrow - 1, m_sem.at[0])
    settle(s_all, wide - 1, s_sem.at[0])

    def given():
        settle(p_all, devices - 1, g_sem.at[0])

    if owners == devices:
        given()
    else:
        pl.when(own < owners)(given)


def write_out(in_a, in_b, in_c, out_a, out_b, out_c, sems):
    copies = [
        pltpu.make_async_copy(src, dst, sems.at[at])
        for at, (src, dst) in enumerate(((in_a, out_a), (in_b, out_b), (in_c, out_c)))
    ]
    for copy in copies:
        copy.start()
    for copy in copies:
        copy.wait()


def on_device(wide, narrow, tensor, factor_a, factor_b, factor_c):
    k_local, i_local, j_whole = tensor.shape
    rank, j_local = factor_b.shape
    flattened = tensor.reshape(k_local * i_local, j_whole)
    vmem = pl.BlockSpec(memory_space=pltpu.VMEM)
    anywhere = pl.BlockSpec(memory_space=pltpu.HBM)
    pair = pltpu.SemaphoreType.DMA((2,))
    f32, bf16 = jnp.float32, jnp.bfloat16
    owners = min(rank, wide * narrow)
    rows = rank // owners
    shapes = (
        jax.ShapeDtypeStruct((rank, i_local), f32),
        jax.ShapeDtypeStruct((rank, j_local), f32),
        jax.ShapeDtypeStruct((k_local, rank), f32),
    )
    steps = pl.pallas_call(
        functools.partial(kernel, wide, narrow, k_local),
        out_shape=shapes,
        in_specs=[anywhere] * 4,
        out_specs=(vmem, vmem, vmem),
        scratch_shapes=[
            pltpu.VMEM((k_local * i_local, j_whole), bf16),
            pltpu.VMEM((rank, i_local), bf16),
            pltpu.VMEM((rank, j_local), bf16),
            pltpu.VMEM((k_local, rank), bf16),
            pltpu.VMEM((wide, rank, j_local), bf16),
            pltpu.VMEM((wide, rank, j_local), bf16),
            pltpu.VMEM((wide, rank, j_local), bf16),
            pltpu.VMEM((owners, rows, 128), f32),
            pltpu.VMEM((wide * narrow, rows, 128), f32),
            pltpu.VMEM((owners, rows, 128), f32),
            pltpu.VMEM((2, rank, 128), f32),
            pltpu.VMEM((narrow, 2, rank, 128), f32),
            pltpu.VMEM((wide, 1, 128), f32),
            pltpu.SemaphoreType.DMA((4,)),
            pair, pair, pair, pair, pair, pair,
        ],
        compiler_params=pltpu.CompilerParams(collective_id=0, has_side_effects=True),
    )(flattened, factor_a, factor_b, factor_c.T)
    step_a, step_b, step_c = pl.pallas_call(
        write_out,
        out_shape=shapes,
        in_specs=[pl.BlockSpec(memory_space=pl.ANY)] * 3,
        out_specs=(anywhere,) * 3,
        scratch_shapes=[pltpu.SemaphoreType.DMA((3,))],
    )(*steps)
    return step_a, step_b, step_c.T


def solution(mesh):
    placed = (P("narrow", "wide", None), P(None, "wide"), P(None, "wide"), P(None, "narrow"))
    return jax.shard_map(
        functools.partial(on_device, mesh.shape["wide"], mesh.shape["narrow"]),
        mesh=mesh,
        in_specs=placed,
        out_specs=(P(None, "wide"), P(None, "wide"), P(None, "narrow")),
        check_vma=False,
    )
```

```python
import functools

import jax
import jax.numpy as jnp
from jax import lax
from jax.experimental import pallas as pl
from jax.experimental.pallas import tpu as pltpu
from jax.sharding import PartitionSpec as P

MESH = pl.DeviceIdType.MESH
highest = lax.Precision.HIGHEST
damping = 1.0


def mm(left, right):
    return jnp.dot(left, right, precision=highest, preferred_element_type=jnp.float32)


def nt(left, right, precision=highest):
    return lax.dot_general(
        left, right, (((1,), (1,)), ((), ())), precision=precision, preferred_element_type=jnp.float32
    )


def total(value):
    return jnp.sum(jnp.sum(value, axis=0, keepdims=True), axis=1, keepdims=True)


def spread(first, last, body):
    if last - first <= 32:
        for step in range(first, last):
            body(step)
        return

    def turn(step, carry):
        body(step)
        return carry

    lax.fori_loop(first, last, turn, 0)


def kernel(
    wide, narrow, k_local, t_hbm, a_hbm, b_hbm, c_hbm, out_a, out_b, out_c,
    t_ref, a_ref, b_ref, c_ref, a_all, c_all, b_all, pb_send, pb_all, p_send, p_all, g_all, m_send, m_all, s_all,
    load_sem, a_sem, c_sem, b_sem, pb_sem, p_sem, g_sem, m_sem, s_sem,
):
    me = lax.axis_index("wide")
    row = lax.axis_index("narrow")
    devices = wide * narrow
    own = row * wide + me
    owners, rows = p_send.shape[0], p_send.shape[1]
    rank, i_local = a_ref.shape
    j_local = b_ref.shape[1]
    k_whole = narrow * k_local

    loads = [
        pltpu.make_async_copy(src, dst, load_sem.at[at])
        for at, (src, dst) in enumerate(
            ((b_hbm, b_ref), (c_hbm, c_ref), (a_hbm, a_ref), (t_hbm, t_ref))
        )
    ]
    for load in loads:
        load.start()

    def wide_peer(step):
        return lax.rem(me + step, wide)

    def device_of(position):
        return lax.rem(position, wide), position // wide

    barrier = pltpu.get_barrier_semaphore()

    def greet(step):
        pl.semaphore_signal(
            barrier, inc=1, device_id=device_of(lax.rem(own + step, devices)), device_id_type=MESH
        )

    spread(1, devices, greet)
    for load in loads[:3]:
        load.wait()
    b_all[me] = b_ref[...]
    a_all[me] = a_ref[...]
    c_all[row] = c_ref[...]
    fa = a_ref[...].astype(jnp.float32)
    eye = jnp.where(
        lax.broadcasted_iota(jnp.int32, (rank, rank), 0)
        == lax.broadcasted_iota(jnp.int32, (rank, rank), 1),
        1.0,
        0.0,
    )
    fc = nt(eye.astype(jnp.bfloat16), c_ref[...], None)
    a_rep = jnp.concatenate([fa] * k_local, axis=1)
    c_rep = jnp.concatenate(
        [jnp.broadcast_to(fc[:, k : k + 1], (rank, i_local)) for k in range(k_local)], axis=1
    )
    khatri = (a_rep * c_rep).astype(jnp.bfloat16)
    lane_k = lax.broadcasted_iota(jnp.int32, (rank, k_local * i_local), 0)
    from_k = lax.broadcasted_iota(jnp.int32, (rank, k_local * i_local), 1) // i_local
    gather_k = jnp.where(lane_k == from_k + row * k_local, 1.0, 0.0)
    pl.semaphore_wait(barrier, devices - 1)

    def send(src, dst, sems, device):
        pltpu.make_async_remote_copy(
            src_ref=src, dst_ref=dst, send_sem=sems.at[0], recv_sem=sems.at[1],
            device_id=device, device_id_type=MESH,
        ).start()

    def settle(buffer, count, sem):
        if count > 0:
            part = buffer.at[pl.ds(0, count)]
            pltpu.make_async_copy(part, part, sem).wait()

    def send_b(step):
        send(b_ref, b_all.at[me], b_sem, (wide_peer(step), row))

    spread(1, wide, send_b)

    def send_c(step):
        there = lax.rem(row + step, narrow)
        send(c_ref, c_all.at[row], c_sem, (me, there))

    spread(1, narrow, send_c)

    def send_a(step):
        send(a_ref, a_all.at[me], a_sem, (wide_peer(step), row))

    spread(1, wide, send_a)

    loads[3].wait()
    partial_b = jnp.dot(khatri, t_ref[...], preferred_element_type=jnp.float32).astype(jnp.bfloat16)
    for w in range(wide):
        pb_send[w] = partial_b[:, w * j_local : (w + 1) * j_local]

    def send_pb(step):
        there = wide_peer(step)
        send(pb_send.at[there], pb_all.at[me], pb_sem, (there, row))

    spread(1, wide, send_pb)
    pb_all[me] = pb_send[me]

    settle(b_all, wide - 1, b_sem.at[1])
    factor_b = jnp.concatenate([b_all[w] for w in range(wide)], axis=1)
    contracted = nt(factor_b, t_ref[...], None)
    weighted = c_rep * contracted
    part_a = weighted[:, :i_local]
    for k in range(1, k_local):
        part_a = part_a + weighted[:, k * i_local : (k + 1) * i_local]
    pair_a = nt(a_rep, weighted)
    pair_b = nt(contracted, khatri.astype(jnp.float32))
    product = a_rep * contracted
    pair_c = nt(c_rep, product)
    column_c = nt(product, gather_k)
    small = jnp.concatenate([pair_a, pair_b, pair_c, column_c], axis=1)
    p_send[...] = small.reshape(owners, rows, 128)

    def send_p(step):
        owner = lax.rem(own + step, owners)

        def go():
            send(p_send.at[owner], p_all.at[own], p_sem, device_of(owner))

        if owners == devices:
            go()
        else:
            pl.when(owner != own)(go)

    spread(1 if owners == devices else 0, owners, send_p)
    settle(a_all, wide - 1, a_sem.at[1])
    settle(c_all, narrow - 1, c_sem.at[1])
    gram_a = nt(a_all[0], a_all[0], None)
    for w in range(1, wide):
        gram_a = gram_a + nt(a_all[w], a_all[w], None)
    whole_c = jnp.concatenate(
        [nt(eye.astype(jnp.bfloat16), c_all[n], None) for n in range(narrow)], axis=1
    )

    def give():
        p_all[own] = p_send[own]
        settle(p_all, devices - 1, p_sem.at[1])
        g_all[own] = jnp.sum(p_all[...], axis=0)

        def send_g(step):
            there = lax.rem(own + step, devices)
            send(g_all.at[own], g_all.at[own], g_sem, device_of(there))

        spread(1, devices, send_g)

    def taken():
        settle(g_all, owners - 1, g_sem.at[1])
        settle(p_all, owners - 1, p_sem.at[0])

    def taken_whole():
        settle(g_all, owners, g_sem.at[1])
        settle(p_all, owners, p_sem.at[0])

    if owners == devices:
        give()
    else:
        pl.when(own < owners)(give)

    settle(pb_all, wide - 1, pb_sem.at[1])
    part_b = jnp.sum(pb_all[...].astype(jnp.float32), axis=0)
    m_send[0] = part_b
    m_send[1, :, :i_local] = part_a
    m_all[row] = m_send[...]

    def send_m(step):
        there = lax.rem(row + step, narrow)
        send(m_send, m_all.at[row], m_sem, (me, there))

    spread(1, narrow, send_m)
    gram_b = nt(factor_b, factor_b, None)
    gram_c = nt(whole_c, whole_c)
    had_a = gram_b * gram_c
    had_b = gram_a * gram_c
    had_c = gram_a * gram_b
    fb = b_ref[...].astype(jnp.float32)
    model_a, model_b, model_c = mm(had_a, fa), mm(had_b, fb), mm(had_c, whole_c)
    inner_a, inner_b, inner_c = mm(gram_a, had_a), mm(gram_b, had_b), mm(gram_c, had_c)
    settle(m_all, narrow - 1, m_sem.at[1])
    summed = jnp.sum(m_all[...], axis=0)
    grad_a = summed[1][:, :i_local] - model_a
    grad_b = summed[0] - model_b

    if owners == devices:
        taken()
    else:
        pl.when(own < owners)(taken)
        pl.when(own >= owners)(taken_whole)
    small = g_all[...].reshape(rank, 128)
    cross_a = small[:, :rank] - inner_a
    cross_b = small[:, rank : 2 * rank] - inner_b
    cross_c = small[:, 2 * rank : 3 * rank] - inner_c
    grad_c = small[:, 3 * rank : 3 * rank + k_whole] - model_c
    mixed_a = cross_b * gram_c + gram_b * cross_c
    mixed_b = cross_a * gram_c + gram_a * cross_c
    mixed_c = cross_a * gram_b + gram_a * cross_b

    had_grad_a = mm(had_a, grad_a)
    had_grad_b = mm(had_b, grad_b)
    had_grad_c = mm(had_c, grad_c)
    image_a = had_grad_a + mm(mixed_a, fa) + damping * grad_a
    image_b = had_grad_b + mm(mixed_b, fb) + damping * grad_b
    image_c = had_grad_c + mm(mixed_c, whole_c) + damping * grad_c
    sums = (
        total(grad_a * grad_a) + total(grad_b * grad_b),
        total(grad_a * had_grad_a) + total(grad_b * had_grad_b),
        total(image_a * image_a) + total(image_b * image_b),
        total(image_a * mm(had_a, image_a)) + total(image_b * mm(had_b, image_b)),
    )
    place = lax.broadcasted_iota(jnp.int32, (1, 128), 1)
    tile = jnp.zeros((1, 128), jnp.float32)
    for at, value in enumerate(sums):
        tile = jnp.where(place == at, value, tile)
    s_all[me] = tile

    def send_s(step):
        send(s_all.at[me], s_all.at[me], s_sem, (wide_peer(step), row))

    spread(1, wide, send_s)

    next_a = mm(cross_a, had_a) + damping * cross_a + nt(gram_a, mixed_a)
    next_b = mm(cross_b, had_b) + damping * cross_b + nt(gram_b, mixed_b)
    next_c = nt(whole_c, image_c)
    later_a = next_b * gram_c + gram_b * next_c
    later_b = next_a * gram_c + gram_a * next_c
    later_c = next_a * gram_b + gram_a * next_b
    known_gg = total(grad_c * grad_c)
    known_gh = total(grad_c * had_grad_c) + total(
        mixed_a * cross_a.T + mixed_b * cross_b.T + mixed_c * cross_c.T
    )
    known_qq = total(image_c * image_c)
    known_qh = total(image_c * mm(had_c, image_c)) + total(
        later_a * next_a.T + later_b * next_b.T + later_c * next_c.T
    )

    settle(s_all, wide - 1, s_sem.at[1])
    tile = jnp.sum(s_all[...], axis=0)
    norm_0 = tile[:, 0:1] + known_gg
    curve_0 = tile[:, 1:2] + known_gh + damping * norm_0
    image_2 = tile[:, 2:3] + known_qq
    image_3 = tile[:, 3:4] + known_qh + damping * image_2

    alpha_0 = norm_0 / curve_0
    norm_1 = norm_0 - 2.0 * alpha_0 * curve_0 + alpha_0 * alpha_0 * image_2
    beta = norm_1 / norm_0
    gain = 1.0 + beta
    curve_1 = gain * gain * curve_0 - 2.0 * gain * alpha_0 * image_2 + alpha_0 * alpha_0 * image_3
    alpha_1 = norm_1 / curve_1
    on_grad = alpha_0 + alpha_1 * gain
    on_image = -alpha_1 * alpha_0
    out_a[...] = on_grad * grad_a + on_image * image_a
    out_b[...] = on_grad * grad_b + on_image * image_b
    step_c = on_grad * grad_c + on_image * image_c
    chosen = jnp.where(
        lax.broadcasted_iota(jnp.int32, (k_local, k_whole), 1)
        == lax.broadcasted_iota(jnp.int32, (k_local, k_whole), 0) + row * k_local,
        1.0,
        0.0,
    )
    out_c[...] = nt(chosen, step_c)

    settle(a_all, wide - 1, a_sem.at[0])
    settle(c_all, narrow - 1, c_sem.at[0])
    settle(b_all, wide - 1, b_sem.at[0])
    settle(pb_all, wide - 1, pb_sem.at[0])
    settle(m_all, narrow - 1, m_sem.at[0])
    settle(s_all, wide - 1, s_sem.at[0])

    def given():
        settle(p_all, devices - 1, g_sem.at[0])

    if owners == devices:
        given()
    else:
        pl.when(own < owners)(given)


def on_device(wide, narrow, tensor, factor_a, factor_b, factor_c):
    k_local, i_local, j_whole = tensor.shape
    rank, j_local = factor_b.shape
    flattened = tensor.reshape(k_local * i_local, j_whole)
    vmem = pl.BlockSpec(memory_space=pltpu.VMEM)
    anywhere = pl.BlockSpec(memory_space=pltpu.HBM)
    pair = pltpu.SemaphoreType.DMA((2,))
    f32, bf16 = jnp.float32, jnp.bfloat16
    owners = min(rank, wide * narrow)
    rows = rank // owners
    shapes = (
        jax.ShapeDtypeStruct((rank, i_local), f32),
        jax.ShapeDtypeStruct((rank, j_local), f32),
        jax.ShapeDtypeStruct((k_local, rank), f32),
    )
    step_a, step_b, step_c = pl.pallas_call(
        functools.partial(kernel, wide, narrow, k_local),
        out_shape=shapes,
        in_specs=[anywhere] * 4,
        out_specs=(vmem, vmem, vmem),
        scratch_shapes=[
            pltpu.VMEM((k_local * i_local, j_whole), bf16),
            pltpu.VMEM((rank, i_local), bf16),
            pltpu.VMEM((rank, j_local), bf16),
            pltpu.VMEM((k_local, rank), bf16),
            pltpu.VMEM((wide, rank, i_local), bf16),
            pltpu.VMEM((narrow, k_local, rank), bf16),
            pltpu.VMEM((wide, rank, j_local), bf16),
            pltpu.VMEM((wide, rank, j_local), bf16),
            pltpu.VMEM((wide, rank, j_local), bf16),
            pltpu.VMEM((owners, rows, 128), f32),
            pltpu.VMEM((wide * narrow, rows, 128), f32),
            pltpu.VMEM((owners, rows, 128), f32),
            pltpu.VMEM((2, rank, 128), f32),
            pltpu.VMEM((narrow, 2, rank, 128), f32),
            pltpu.VMEM((wide, 1, 128), f32),
            pltpu.SemaphoreType.DMA((4,)),
            pair, pair, pair, pair, pair, pair, pair, pair,
        ],
        compiler_params=pltpu.CompilerParams(collective_id=0, has_side_effects=True),
    )(flattened, factor_a, factor_b, factor_c.T)
    return step_a, step_b, step_c.T


def solution(mesh):
    placed = (P("narrow", "wide", None), P(None, "wide"), P(None, "wide"), P(None, "narrow"))
    return jax.shard_map(
        functools.partial(on_device, mesh.shape["wide"], mesh.shape["narrow"]),
        mesh=mesh,
        in_specs=placed,
        out_specs=(P(None, "wide"), P(None, "wide"), P(None, "narrow")),
        check_vma=False,
    )
```

```python
import functools

import jax
import jax.numpy as jnp
from jax import lax
from jax.experimental import pallas as pl
from jax.experimental.pallas import tpu as pltpu
from jax.sharding import PartitionSpec as P

MESH = pl.DeviceIdType.MESH
highest = lax.Precision.HIGHEST
damping = 1.0


def mm(left, right):
    return jnp.dot(left, right, precision=highest, preferred_element_type=jnp.float32)


def nt(left, right, precision=highest):
    return lax.dot_general(
        left, right, (((1,), (1,)), ((), ())), precision=precision, preferred_element_type=jnp.float32
    )


def total(value):
    return jnp.sum(jnp.sum(value, axis=0, keepdims=True), axis=1, keepdims=True)


def spread(first, last, body):
    if last - first <= 32:
        for step in range(first, last):
            body(step)
        return

    def turn(step, carry):
        body(step)
        return carry

    lax.fori_loop(first, last, turn, 0)


def kernel(
    wide, narrow, k_local, t_hbm, a_hbm, b_hbm, c_hbm, out_a, out_b, out_c,
    t_ref, a_ref, b_ref, c_ref, c_all, b_all, pb_send, pb_half, pb_all, p_send, p_all, w_all, g_all,
    m_send, m_all, s_all,
    load_sem, c_sem, b_sem, relay_sem, half_sem, pb_sem, p_sem, w_sem, g_sem, m_sem, s_sem,
):
    me = lax.axis_index("wide")
    row = lax.axis_index("narrow")
    core = lax.rem(me, 2)
    chip = me // 2
    chips = wide // 2
    quad = 2 * narrow
    mine = row * 2 + core
    partner = (chip * 2 + 1 - core, row)
    rank, i_local = a_ref.shape
    j_local = b_ref.shape[1]
    k_whole = narrow * k_local

    loads = [
        pltpu.make_async_copy(src, dst, load_sem.at[at])
        for at, (src, dst) in enumerate(
            ((b_hbm, b_ref), (c_hbm, c_ref), (a_hbm, a_ref), (t_hbm, t_ref))
        )
    ]
    for load in loads:
        load.start()

    def wide_peer(step):
        return lax.rem(me + step, wide)

    def chip_peer(step):
        return lax.rem(chip + step, chips)

    def quad_peer(step):
        other = lax.rem(mine + step, quad)
        return other, (chip * 2 + lax.rem(other, 2), other // 2)

    barrier = pltpu.get_barrier_semaphore()

    def greet(step):
        pl.semaphore_signal(barrier, inc=1, device_id=(wide_peer(step), row), device_id_type=MESH)

    def greet_row(step):
        there = lax.rem(row + step, narrow)
        for side in range(2):
            pl.semaphore_signal(
                barrier, inc=1, device_id=(chip * 2 + side, there), device_id_type=MESH
            )

    spread(1, wide, greet)
    spread(1, narrow, greet_row)
    for load in loads[:3]:
        load.wait()
    b_all[core, chip] = b_ref[...]
    c_all[row] = c_ref[...]
    fa = a_ref[...].astype(jnp.float32)
    eye = jnp.where(
        lax.broadcasted_iota(jnp.int32, (rank, rank), 0)
        == lax.broadcasted_iota(jnp.int32, (rank, rank), 1),
        1.0,
        0.0,
    )
    fc = nt(eye.astype(jnp.bfloat16), c_ref[...], None)
    a_rep = jnp.concatenate([fa] * k_local, axis=1)
    c_rep = jnp.concatenate(
        [jnp.broadcast_to(fc[:, k : k + 1], (rank, i_local)) for k in range(k_local)], axis=1
    )
    khatri = (a_rep * c_rep).astype(jnp.bfloat16)
    lane_k = lax.broadcasted_iota(jnp.int32, (rank, k_local * i_local), 0)
    from_k = lax.broadcasted_iota(jnp.int32, (rank, k_local * i_local), 1) // i_local
    gather_k = jnp.where(lane_k == from_k + row * k_local, 1.0, 0.0)
    gram_a_own = nt(a_ref[...], a_ref[...], None) * jnp.where(row == 0, 1.0, 0.0)
    pl.semaphore_wait(barrier, (wide - 1) + 2 * (narrow - 1))

    def send(src, dst, sems, device):
        pltpu.make_async_remote_copy(
            src_ref=src, dst_ref=dst, send_sem=sems.at[0], recv_sem=sems.at[1],
            device_id=device, device_id_type=MESH,
        ).start()

    def settle(buffer, count, sem):
        if count > 0:
            part = buffer.at[pl.ds(0, count)]
            pltpu.make_async_copy(part, part, sem).wait()

    def send_b(step):
        send(b_ref, b_all.at[core, chip], b_sem, (chip_peer(step) * 2 + core, row))

    spread(1, chips, send_b)

    def send_c(step):
        there = lax.rem(row + step, narrow)
        send(c_ref, c_all.at[row], c_sem, (me, there))

    spread(1, narrow, send_c)

    loads[3].wait()
    partial_b = jnp.dot(khatri, t_ref[...], preferred_element_type=jnp.float32)
    for w in range(wide):
        pb_send[w % 2, w // 2] = partial_b[:, w * j_local : (w + 1) * j_local]
    send(pb_send.at[1 - core], pb_half, half_sem, partner)

    def contract(side):
        blocks = jnp.concatenate([b_all[side, at] for at in range(chips)], axis=1)
        columns = [
            t_ref[:, pl.ds(pl.multiple_of((at * 2 + side) * j_local, j_local), j_local)]
            for at in range(chips)
        ]
        return nt(blocks, jnp.concatenate(columns, axis=1), None)

    settle(b_all.at[core], chips - 1, b_sem.at[1])
    send(b_all.at[core], b_all.at[core], relay_sem, partner)
    contracted = contract(core)
    settle(pb_half, chips, half_sem.at[1])
    for at in range(chips):
        pb_half[at] = pb_half[at] + pb_send[core, at]

    def send_pb(step):
        there = chip_peer(step)
        send(pb_half.at[there], pb_all.at[chip], pb_sem, (there * 2 + core, row))

    spread(1, chips, send_pb)
    pb_all[chip] = pb_half[chip]
    settle(b_all.at[1 - core], chips, relay_sem.at[1])
    contracted = contracted + contract(1 - core)
    weighted = c_rep * contracted
    part_a = weighted[:, :i_local]
    for k in range(1, k_local):
        part_a = part_a + weighted[:, k * i_local : (k + 1) * i_local]
    pair_a = nt(a_rep, weighted)
    pair_b = nt(contracted, khatri.astype(jnp.float32))
    product = a_rep * contracted
    column_c = nt(product, gather_k)
    small = jnp.concatenate([pair_a, pair_b, gram_a_own, column_c], axis=1)
    p_send[...] = small.reshape(p_send.shape)

    def send_p(step):
        other, there = quad_peer(step)
        send(p_send.at[other], p_all.at[mine], p_sem, there)

    spread(1, quad, send_p)
    p_all[mine] = p_send[mine]
    settle(c_all, narrow - 1, c_sem.at[1])
    whole_c = jnp.concatenate(
        [nt(eye.astype(jnp.bfloat16), c_all[n], None) for n in range(narrow)], axis=1
    )
    settle(p_all, quad - 1, p_sem.at[1])
    w_all[chip] = jnp.sum(p_all[...], axis=0)

    def send_w(step):
        send(w_all.at[chip], w_all.at[chip], w_sem, (chip_peer(step) * 2 + core, row))

    spread(1, chips, send_w)

    settle(pb_all, chips - 1, pb_sem.at[1])
    part_b = jnp.sum(pb_all[...], axis=0)
    m_send[0] = part_b
    m_send[1, :, :i_local] = part_a
    m_all[row] = m_send[...]

    def send_m(step):
        there = lax.rem(row + step, narrow)
        send(m_send, m_all.at[row], m_sem, (me, there))

    spread(1, narrow, send_m)
    factor_b = jnp.concatenate([b_all[w % 2, w // 2] for w in range(wide)], axis=1)
    gram_b = nt(factor_b, factor_b, None)
    gram_c = nt(whole_c, whole_c)
    had_a = gram_b * gram_c
    settle(w_all, chips - 1, w_sem.at[1])
    g_all[mine] = jnp.sum(w_all[...], axis=0)

    def send_g(step):
        other, there = quad_peer(step)
        send(g_all.at[mine], g_all.at[mine], g_sem, there)

    spread(1, quad, send_g)
    fb = b_ref[...].astype(jnp.float32)
    model_a = mm(had_a, fa)
    settle(m_all, narrow - 1, m_sem.at[1])
    summed = jnp.sum(m_all[...], axis=0)
    grad_a = summed[1][:, :i_local] - model_a
    had_grad_a = mm(had_a, grad_a)

    settle(g_all, quad - 1, g_sem.at[1])
    small = g_all[...].reshape(rank, 128)
    gram_a = small[:, 2 * rank : 3 * rank]
    mttkrp_c = small[:, 3 * rank : 3 * rank + k_whole]
    had_b = gram_a * gram_c
    had_c = gram_a * gram_b
    cross_a = small[:, :rank] - mm(gram_a, had_a)
    cross_b = small[:, rank : 2 * rank] - mm(gram_b, had_b)
    cross_c = nt(whole_c, mttkrp_c) - mm(gram_c, had_c)
    grad_b = summed[0] - mm(had_b, fb)
    grad_c = mttkrp_c - mm(had_c, whole_c)
    mixed_a = cross_b * gram_c + gram_b * cross_c
    mixed_b = cross_a * gram_c + gram_a * cross_c
    mixed_c = cross_a * gram_b + gram_a * cross_b

    had_grad_b = mm(had_b, grad_b)
    had_grad_c = mm(had_c, grad_c)
    image_a = had_grad_a + mm(mixed_a, fa) + damping * grad_a
    image_b = had_grad_b + mm(mixed_b, fb) + damping * grad_b
    image_c = had_grad_c + mm(mixed_c, whole_c) + damping * grad_c
    sums = (
        total(grad_a * grad_a) + total(grad_b * grad_b),
        total(grad_a * had_grad_a) + total(grad_b * had_grad_b),
        total(image_a * image_a) + total(image_b * image_b),
        total(image_a * mm(had_a, image_a)) + total(image_b * mm(had_b, image_b)),
    )
    place = lax.broadcasted_iota(jnp.int32, (1, 128), 1)
    tile = jnp.zeros((1, 128), jnp.float32)
    for at, value in enumerate(sums):
        tile = jnp.where(place == at, value, tile)
    s_all[me] = tile

    def send_s(step):
        send(s_all.at[me], s_all.at[me], s_sem, (wide_peer(step), row))

    spread(1, wide, send_s)

    next_a = mm(cross_a, had_a) + damping * cross_a + nt(gram_a, mixed_a)
    next_b = mm(cross_b, had_b) + damping * cross_b + nt(gram_b, mixed_b)
    next_c = nt(whole_c, image_c)
    later_a = next_b * gram_c + gram_b * next_c
    later_b = next_a * gram_c + gram_a * next_c
    later_c = next_a * gram_b + gram_a * next_b
    known_gg = total(grad_c * grad_c)
    known_gh = total(grad_c * had_grad_c) + total(
        mixed_a * cross_a.T + mixed_b * cross_b.T + mixed_c * cross_c.T
    )
    known_qq = total(image_c * image_c)
    known_qh = total(image_c * mm(had_c, image_c)) + total(
        later_a * next_a.T + later_b * next_b.T + later_c * next_c.T
    )

    settle(s_all, wide - 1, s_sem.at[1])
    tile = jnp.sum(s_all[...], axis=0)
    norm_0 = tile[:, 0:1] + known_gg
    curve_0 = tile[:, 1:2] + known_gh + damping * norm_0
    image_2 = tile[:, 2:3] + known_qq
    image_3 = tile[:, 3:4] + known_qh + damping * image_2

    alpha_0 = norm_0 / curve_0
    norm_1 = norm_0 - 2.0 * alpha_0 * curve_0 + alpha_0 * alpha_0 * image_2
    beta = norm_1 / norm_0
    gain = 1.0 + beta
    curve_1 = gain * gain * curve_0 - 2.0 * gain * alpha_0 * image_2 + alpha_0 * alpha_0 * image_3
    alpha_1 = norm_1 / curve_1
    on_grad = alpha_0 + alpha_1 * gain
    on_image = -alpha_1 * alpha_0
    out_a[...] = on_grad * grad_a + on_image * image_a
    out_b[...] = on_grad * grad_b + on_image * image_b
    step_c = on_grad * grad_c + on_image * image_c
    chosen = jnp.where(
        lax.broadcasted_iota(jnp.int32, (k_whole, k_local), 0)
        == lax.broadcasted_iota(jnp.int32, (k_whole, k_local), 1) + row * k_local,
        1.0,
        0.0,
    )
    out_c[...] = mm(step_c, chosen)

    settle(c_all, narrow - 1, c_sem.at[0])
    settle(b_all.at[0], chips - 1, b_sem.at[0])
    settle(b_all.at[0], chips, relay_sem.at[0])
    settle(pb_half, chips, half_sem.at[0])
    settle(pb_all, chips - 1, pb_sem.at[0])
    settle(p_all, quad - 1, p_sem.at[0])
    settle(w_all, chips - 1, w_sem.at[0])
    settle(g_all, quad - 1, g_sem.at[0])
    settle(m_all, narrow - 1, m_sem.at[0])
    settle(s_all, wide - 1, s_sem.at[0])


def on_device(wide, narrow, tensor, factor_a, factor_b, factor_c):
    k_local, i_local, j_whole = tensor.shape
    rank, j_local = factor_b.shape
    flattened = tensor.reshape(k_local * i_local, j_whole)
    vmem = pl.BlockSpec(memory_space=pltpu.VMEM)
    anywhere = pl.BlockSpec(memory_space=pltpu.HBM)
    pair = pltpu.SemaphoreType.DMA((2,))
    f32, bf16 = jnp.float32, jnp.bfloat16
    chips, quad = wide // 2, 2 * narrow
    rows = rank // quad
    shapes = (
        jax.ShapeDtypeStruct((rank, i_local), f32),
        jax.ShapeDtypeStruct((rank, j_local), f32),
        jax.ShapeDtypeStruct((rank, k_local), f32),
    )
    step_a, step_b, step_c = pl.pallas_call(
        functools.partial(kernel, wide, narrow, k_local),
        out_shape=shapes,
        in_specs=[anywhere] * 4,
        out_specs=(vmem, vmem, vmem),
        scratch_shapes=[
            pltpu.VMEM((k_local * i_local, j_whole), bf16),
            pltpu.VMEM((rank, i_local), bf16),
            pltpu.VMEM((rank, j_local), bf16),
            pltpu.VMEM((k_local, rank), bf16),
            pltpu.VMEM((narrow, k_local, rank), bf16),
            pltpu.VMEM((2, chips, rank, j_local), bf16),
            pltpu.VMEM((2, chips, rank, j_local), f32),
            pltpu.VMEM((chips, rank, j_local), f32),
            pltpu.VMEM((chips, rank, j_local), f32),
            pltpu.VMEM((quad, rows, 128), f32),
            pltpu.VMEM((quad, rows, 128), f32),
            pltpu.VMEM((chips, rows, 128), f32),
            pltpu.VMEM((quad, rows, 128), f32),
            pltpu.VMEM((2, rank, 128), f32),
            pltpu.VMEM((narrow, 2, rank, 128), f32),
            pltpu.VMEM((wide, 1, 128), f32),
            pltpu.SemaphoreType.DMA((4,)),
            pair, pair, pair, pair, pair, pair, pair, pair, pair, pair,
        ],
        compiler_params=pltpu.CompilerParams(collective_id=0, has_side_effects=True),
    )(flattened, factor_a, factor_b, factor_c.T)
    return step_a, step_b, step_c


def solution(mesh):
    placed = (P("narrow", "wide", None), P(None, "wide"), P(None, "wide"), P(None, "narrow"))
    return jax.shard_map(
        functools.partial(on_device, mesh.shape["wide"], mesh.shape["narrow"]),
        mesh=mesh,
        in_specs=placed,
        out_specs=(P(None, "wide"), P(None, "wide"), P(None, "narrow")),
        check_vma=False,
    )
```

```python
import functools

import jax
import jax.numpy as jnp
from jax import lax
from jax.experimental import pallas as pl
from jax.experimental.pallas import tpu as pltpu
from jax.sharding import PartitionSpec as P

MESH = pl.DeviceIdType.MESH
highest = lax.Precision.HIGHEST
damping = 1.0


def mm(left, right):
    return jnp.dot(left, right, precision=highest, preferred_element_type=jnp.float32)


def nt(left, right, precision=highest):
    return lax.dot_general(
        left, right, (((1,), (1,)), ((), ())), precision=precision, preferred_element_type=jnp.float32
    )


def total(value):
    return jnp.sum(jnp.sum(value, axis=0, keepdims=True), axis=1, keepdims=True)


def spread(first, last, body):
    if last - first <= 32:
        for step in range(first, last):
            body(step)
        return

    def turn(step, carry):
        body(step)
        return carry

    lax.fori_loop(first, last, turn, 0)


def kernel(
    wide, narrow, k_local, t_hbm, a_hbm, b_hbm, c_hbm, out_a, out_b, out_c,
    t_ref, a_ref, b_ref, c_ref, c_all, b_all, pb_send, pb_half, pb_all, p_all, w_all,
    m_send, m_all, s_all,
    load_sem, c_sem, b_sem, cross_sem, half_sem, pb_sem, p_sem, w_sem, m_sem, s_sem,
):
    me = lax.axis_index("wide")
    row = lax.axis_index("narrow")
    core = lax.rem(me, 2)
    chip = me // 2
    chips = wide // 2
    low = 4 if wide % 4 == 0 else 2
    high = wide // low
    group = low * narrow
    layer, side_low = me // low, lax.rem(me, low)
    mine = row * low + side_low
    partner = (chip * 2 + 1 - core, row)
    rank, i_local = a_ref.shape
    j_local = b_ref.shape[1]
    k_whole = narrow * k_local

    loads = [
        pltpu.make_async_copy(src, dst, load_sem.at[at])
        for at, (src, dst) in enumerate(
            ((b_hbm, b_ref), (c_hbm, c_ref), (a_hbm, a_ref), (t_hbm, t_ref))
        )
    ]
    for load in loads:
        load.start()

    def wide_peer(step):
        return lax.rem(me + step, wide)

    def chip_peer(step):
        return lax.rem(chip + step, chips)

    def group_peer(step):
        other = lax.rem(mine + step, group)
        return layer * low + lax.rem(other, low), other // low

    def layer_peer(step):
        return lax.rem(layer + step, high) * low + side_low, row

    barrier = pltpu.get_barrier_semaphore()

    def greet(step):
        pl.semaphore_signal(barrier, inc=1, device_id=(wide_peer(step), row), device_id_type=MESH)

    def greet_row(step):
        there = lax.rem(row + step, narrow)
        for side in range(low):
            pl.semaphore_signal(
                barrier, inc=1, device_id=(layer * low + side, there), device_id_type=MESH
            )

    spread(1, wide, greet)
    spread(1, narrow, greet_row)
    for load in loads[:3]:
        load.wait()
    b_all[core, chip] = b_ref[...]
    c_all[row] = c_ref[...]
    fa = a_ref[...].astype(jnp.float32)
    eye = jnp.where(
        lax.broadcasted_iota(jnp.int32, (rank, rank), 0)
        == lax.broadcasted_iota(jnp.int32, (rank, rank), 1),
        1.0,
        0.0,
    )
    fc = nt(eye.astype(jnp.bfloat16), c_ref[...], None)
    a_rep = jnp.concatenate([fa] * k_local, axis=1)
    c_rep = jnp.concatenate(
        [jnp.broadcast_to(fc[:, k : k + 1], (rank, i_local)) for k in range(k_local)], axis=1
    )
    khatri = (a_rep * c_rep).astype(jnp.bfloat16)
    lane_k = lax.broadcasted_iota(jnp.int32, (rank, k_local * i_local), 0)
    from_k = lax.broadcasted_iota(jnp.int32, (rank, k_local * i_local), 1) // i_local
    gather_k = jnp.where(lane_k == from_k + row * k_local, 1.0, 0.0)
    gram_a_own = nt(a_ref[...], a_ref[...], None) * jnp.where(row == 0, 1.0, 0.0)
    pl.semaphore_wait(barrier, (wide - 1) + low * (narrow - 1))

    def send(src, dst, sems, device):
        pltpu.make_async_remote_copy(
            src_ref=src, dst_ref=dst, send_sem=sems.at[0], recv_sem=sems.at[1],
            device_id=device, device_id_type=MESH,
        ).start()

    def settle(buffer, count, sem):
        if count > 0:
            part = buffer.at[pl.ds(0, count)]
            pltpu.make_async_copy(part, part, sem).wait()

    def send_b(step):
        send(b_ref, b_all.at[core, chip], b_sem, (chip_peer(step) * 2 + core, row))

    def send_b_across(step):
        there = chip_peer(step) * 2 + 1 - core
        send(b_ref, b_all.at[core, chip], cross_sem, (there, row))

    spread(1, chips, send_b)
    spread(0, chips, send_b_across)

    def send_c(step):
        there = lax.rem(row + step, narrow)
        send(c_ref, c_all.at[row], c_sem, (me, there))

    spread(1, narrow, send_c)

    loads[3].wait()
    partial_b = jnp.dot(khatri, t_ref[...], preferred_element_type=jnp.float32)
    for w in range(wide):
        pb_send[w % 2, w // 2] = partial_b[:, w * j_local : (w + 1) * j_local]
    send(pb_send.at[1 - core], pb_half, half_sem, partner)

    def contract(side):
        blocks = jnp.concatenate([b_all[side, at] for at in range(chips)], axis=1)
        columns = [
            t_ref[:, pl.ds(pl.multiple_of((at * 2 + side) * j_local, j_local), j_local)]
            for at in range(chips)
        ]
        return nt(blocks, jnp.concatenate(columns, axis=1), None)

    settle(b_all.at[core], chips - 1, b_sem.at[1])
    contracted = contract(core)
    settle(pb_half, chips, half_sem.at[1])
    for at in range(chips):
        pb_half[at] = pb_half[at] + pb_send[core, at]

    def send_pb(step):
        there = chip_peer(step)
        send(pb_half.at[there], pb_all.at[chip], pb_sem, (there * 2 + core, row))

    spread(1, chips, send_pb)
    pb_all[chip] = pb_half[chip]
    settle(b_all.at[1 - core], chips, cross_sem.at[1])
    contracted = contracted + contract(1 - core)
    weighted = c_rep * contracted
    part_a = weighted[:, :i_local]
    for k in range(1, k_local):
        part_a = part_a + weighted[:, k * i_local : (k + 1) * i_local]
    pair_a = nt(a_rep, weighted)
    pair_b = nt(contracted, khatri.astype(jnp.float32))
    product = a_rep * contracted
    column_c = nt(product, gather_k)
    p_all[mine] = jnp.concatenate([pair_a, pair_b, gram_a_own, column_c], axis=1)

    def send_p(step):
        send(p_all.at[mine], p_all.at[mine], p_sem, group_peer(step))

    spread(1, group, send_p)
    settle(c_all, narrow - 1, c_sem.at[1])
    whole_c = jnp.concatenate(
        [nt(eye.astype(jnp.bfloat16), c_all[n], None) for n in range(narrow)], axis=1
    )
    settle(p_all, group - 1, p_sem.at[1])
    w_all[layer] = jnp.sum(p_all[...], axis=0)

    def send_w(step):
        send(w_all.at[layer], w_all.at[layer], w_sem, layer_peer(step))

    spread(1, high, send_w)

    settle(pb_all, chips - 1, pb_sem.at[1])
    part_b = jnp.sum(pb_all[...], axis=0)
    m_send[0] = part_b
    m_send[1, :, :i_local] = part_a
    m_all[row] = m_send[...]

    def send_m(step):
        there = lax.rem(row + step, narrow)
        send(m_send, m_all.at[row], m_sem, (me, there))

    spread(1, narrow, send_m)
    factor_b = jnp.concatenate([b_all[w % 2, w // 2] for w in range(wide)], axis=1)
    gram_b = nt(factor_b, factor_b, None)
    gram_c = nt(whole_c, whole_c)
    had_a = gram_b * gram_c
    fb = b_ref[...].astype(jnp.float32)
    model_a = mm(had_a, fa)
    settle(m_all, narrow - 1, m_sem.at[1])
    summed = jnp.sum(m_all[...], axis=0)
    grad_a = summed[1][:, :i_local] - model_a
    had_grad_a = mm(had_a, grad_a)

    settle(w_all, high - 1, w_sem.at[1])
    small = jnp.sum(w_all[...], axis=0)
    gram_a = small[:, 2 * rank : 3 * rank]
    mttkrp_c = small[:, 3 * rank : 3 * rank + k_whole]
    had_b = gram_a * gram_c
    had_c = gram_a * gram_b
    cross_a = small[:, :rank] - mm(gram_a, had_a)
    cross_b = small[:, rank : 2 * rank] - mm(gram_b, had_b)
    cross_c = nt(whole_c, mttkrp_c) - mm(gram_c, had_c)
    grad_b = summed[0] - mm(had_b, fb)
    grad_c = mttkrp_c - mm(had_c, whole_c)
    mixed_a = cross_b * gram_c + gram_b * cross_c
    mixed_b = cross_a * gram_c + gram_a * cross_c
    mixed_c = cross_a * gram_b + gram_a * cross_b

    had_grad_b = mm(had_b, grad_b)
    had_grad_c = mm(had_c, grad_c)
    image_a = had_grad_a + mm(mixed_a, fa) + damping * grad_a
    image_b = had_grad_b + mm(mixed_b, fb) + damping * grad_b
    image_c = had_grad_c + mm(mixed_c, whole_c) + damping * grad_c
    sums = (
        total(grad_a * grad_a) + total(grad_b * grad_b),
        total(grad_a * had_grad_a) + total(grad_b * had_grad_b),
        total(image_a * image_a) + total(image_b * image_b),
        total(image_a * mm(had_a, image_a)) + total(image_b * mm(had_b, image_b)),
    )
    place = lax.broadcasted_iota(jnp.int32, (1, 128), 1)
    tile = jnp.zeros((1, 128), jnp.float32)
    for at, value in enumerate(sums):
        tile = jnp.where(place == at, value, tile)
    s_all[me] = tile

    def send_s(step):
        send(s_all.at[me], s_all.at[me], s_sem, (wide_peer(step), row))

    spread(1, wide, send_s)

    next_a = mm(cross_a, had_a) + damping * cross_a + nt(gram_a, mixed_a)
    next_b = mm(cross_b, had_b) + damping * cross_b + nt(gram_b, mixed_b)
    next_c = nt(whole_c, image_c)
    later_a = next_b * gram_c + gram_b * next_c
    later_b = next_a * gram_c + gram_a * next_c
    later_c = next_a * gram_b + gram_a * next_b
    known_gg = total(grad_c * grad_c)
    known_gh = total(grad_c * had_grad_c) + total(
        mixed_a * cross_a.T + mixed_b * cross_b.T + mixed_c * cross_c.T
    )
    known_qq = total(image_c * image_c)
    known_qh = total(image_c * mm(had_c, image_c)) + total(
        later_a * next_a.T + later_b * next_b.T + later_c * next_c.T
    )

    chosen = jnp.where(
        lax.broadcasted_iota(jnp.int32, (k_local, k_whole), 1)
        == lax.broadcasted_iota(jnp.int32, (k_local, k_whole), 0) + row * k_local,
        1.0,
        0.0,
    )
    own_grad_c, own_image_c = nt(chosen, grad_c), nt(chosen, image_c)

    settle(s_all, wide - 1, s_sem.at[1])
    tile = jnp.sum(s_all[...], axis=0)
    norm_0 = tile[:, 0:1] + known_gg
    curve_0 = tile[:, 1:2] + known_gh + damping * norm_0
    image_2 = tile[:, 2:3] + known_qq
    image_3 = tile[:, 3:4] + known_qh + damping * image_2

    alpha_0 = norm_0 / curve_0
    norm_1 = norm_0 - 2.0 * alpha_0 * curve_0 + alpha_0 * alpha_0 * image_2
    beta = norm_1 / norm_0
    gain = 1.0 + beta
    curve_1 = gain * gain * curve_0 - 2.0 * gain * alpha_0 * image_2 + alpha_0 * alpha_0 * image_3
    alpha_1 = norm_1 / curve_1
    on_grad = alpha_0 + alpha_1 * gain
    on_image = -alpha_1 * alpha_0
    out_a[...] = on_grad * grad_a + on_image * image_a
    out_b[...] = on_grad * grad_b + on_image * image_b
    out_c[...] = on_grad * own_grad_c + on_image * own_image_c

    settle(c_all, narrow - 1, c_sem.at[0])
    settle(b_all.at[0], chips - 1, b_sem.at[0])
    settle(b_all.at[0], chips, cross_sem.at[0])
    settle(pb_half, chips, half_sem.at[0])
    settle(pb_all, chips - 1, pb_sem.at[0])
    settle(p_all, group - 1, p_sem.at[0])
    settle(w_all, high - 1, w_sem.at[0])
    settle(m_all, narrow - 1, m_sem.at[0])
    settle(s_all, wide - 1, s_sem.at[0])


def write_out(in_a, in_b, in_c, out_a, out_b, out_c, sems):
    copies = [
        pltpu.make_async_copy(src, dst, sems.at[at])
        for at, (src, dst) in enumerate(((in_a, out_a), (in_b, out_b), (in_c, out_c)))
    ]
    for copy in copies:
        copy.start()
    for copy in copies:
        copy.wait()


def on_device(wide, narrow, tensor, factor_a, factor_b, factor_c):
    k_local, i_local, j_whole = tensor.shape
    rank, j_local = factor_b.shape
    flattened = tensor.reshape(k_local * i_local, j_whole)
    vmem = pl.BlockSpec(memory_space=pltpu.VMEM)
    anywhere = pl.BlockSpec(memory_space=pltpu.HBM)
    pair = pltpu.SemaphoreType.DMA((2,))
    f32, bf16 = jnp.float32, jnp.bfloat16
    chips = wide // 2
    low = 4 if wide % 4 == 0 else 2
    shapes = (
        jax.ShapeDtypeStruct((rank, i_local), f32),
        jax.ShapeDtypeStruct((rank, j_local), f32),
        jax.ShapeDtypeStruct((k_local, rank), f32),
    )
    steps = pl.pallas_call(
        functools.partial(kernel, wide, narrow, k_local),
        out_shape=shapes,
        in_specs=[anywhere] * 4,
        out_specs=(vmem, vmem, vmem),
        scratch_shapes=[
            pltpu.VMEM((k_local * i_local, j_whole), bf16),
            pltpu.VMEM((rank, i_local), bf16),
            pltpu.VMEM((rank, j_local), bf16),
            pltpu.VMEM((k_local, rank), bf16),
            pltpu.VMEM((narrow, k_local, rank), bf16),
            pltpu.VMEM((2, chips, rank, j_local), bf16),
            pltpu.VMEM((2, chips, rank, j_local), f32),
            pltpu.VMEM((chips, rank, j_local), f32),
            pltpu.VMEM((chips, rank, j_local), f32),
            pltpu.VMEM((low * narrow, rank, 128), f32),
            pltpu.VMEM((wide // low, rank, 128), f32),
            pltpu.VMEM((2, rank, 128), f32),
            pltpu.VMEM((narrow, 2, rank, 128), f32),
            pltpu.VMEM((wide, 1, 128), f32),
            pltpu.SemaphoreType.DMA((4,)),
            pair, pair, pair, pair, pair, pair, pair, pair, pair,
        ],
        compiler_params=pltpu.CompilerParams(collective_id=0, has_side_effects=True),
    )(flattened, factor_a, factor_b, factor_c.T)
    step_a, step_b, step_c = pl.pallas_call(
        write_out,
        out_shape=shapes,
        in_specs=[anywhere] * 3,
        out_specs=(anywhere,) * 3,
        scratch_shapes=[pltpu.SemaphoreType.DMA((3,))],
    )(*steps)
    return step_a, step_b, step_c.T


def solution(mesh):
    placed = (P("narrow", "wide", None), P(None, "wide"), P(None, "wide"), P(None, "narrow"))
    return jax.shard_map(
        functools.partial(on_device, mesh.shape["wide"], mesh.shape["narrow"]),
        mesh=mesh,
        in_specs=placed,
        out_specs=(P(None, "wide"), P(None, "wide"), P(None, "narrow")),
        check_vma=False,
    )
```

```python
import functools

import jax
import jax.numpy as jnp
from jax import lax
from jax.experimental import pallas as pl
from jax.experimental.pallas import tpu as pltpu
from jax.sharding import PartitionSpec as P

MESH = pl.DeviceIdType.MESH
highest = lax.Precision.HIGHEST
damping = 1.0


def mm(left, right):
    return jnp.dot(left, right, precision=highest, preferred_element_type=jnp.float32)


def nt(left, right, precision=highest):
    return lax.dot_general(
        left, right, (((1,), (1,)), ((), ())), precision=precision, preferred_element_type=jnp.float32
    )


def total(value):
    return jnp.sum(jnp.sum(value, axis=0, keepdims=True), axis=1, keepdims=True)


def spread(first, last, body):
    if last - first <= 32:
        for step in range(first, last):
            body(step)
        return

    def turn(step, carry):
        body(step)
        return carry

    lax.fori_loop(first, last, turn, 0)


def kernel(
    wide, narrow, k_local, t_hbm, a_hbm, b_hbm, c_hbm, out_a, out_b, out_c,
    t_ref, a_ref, b_ref, c_ref, c_all, b_all, pb_send, pb_half, pb_all, p_all, w_all,
    m_send, m_all, s_all,
    load_sem, c_sem, b_sem, cross_sem, half_sem, pb_sem, p_sem, w_sem, m_sem, s_sem,
):
    me = lax.axis_index("wide")
    row = lax.axis_index("narrow")
    core = lax.rem(me, 2)
    chip = me // 2
    chips = wide // 2
    low = 4 if wide % 4 == 0 else 2
    high = wide // low
    group = low * narrow
    layer, side_low = me // low, lax.rem(me, low)
    mine = row * low + side_low
    partner = (chip * 2 + 1 - core, row)
    rank, i_local = a_ref.shape
    j_local = b_ref.shape[1]
    k_whole = narrow * k_local

    loads = [
        pltpu.make_async_copy(src, dst, load_sem.at[at])
        for at, (src, dst) in enumerate(
            ((b_hbm, b_ref), (c_hbm, c_ref), (a_hbm, a_ref), (t_hbm, t_ref))
        )
    ]
    for load in loads:
        load.start()

    def wide_peer(step):
        return lax.rem(me + step, wide)

    def chip_peer(step):
        return lax.rem(chip + step, chips)

    def group_peer(step):
        other = lax.rem(mine + step, group)
        return layer * low + lax.rem(other, low), other // low

    def layer_peer(step):
        return lax.rem(layer + step, high) * low + side_low, row

    barrier = pltpu.get_barrier_semaphore()

    def greet(step):
        pl.semaphore_signal(barrier, inc=1, device_id=(wide_peer(step), row), device_id_type=MESH)

    def greet_row(step):
        there = lax.rem(row + step, narrow)
        for side in range(low):
            pl.semaphore_signal(
                barrier, inc=1, device_id=(layer * low + side, there), device_id_type=MESH
            )

    spread(1, wide, greet)
    spread(1, narrow, greet_row)
    loads[0].wait()
    b_all[core, chip] = b_ref[...]
    pl.semaphore_wait(barrier, (wide - 1) + low * (narrow - 1))

    def send(src, dst, sems, device):
        pltpu.make_async_remote_copy(
            src_ref=src, dst_ref=dst, send_sem=sems.at[0], recv_sem=sems.at[1],
            device_id=device, device_id_type=MESH,
        ).start()

    def settle(buffer, count, sem):
        if count > 0:
            part = buffer.at[pl.ds(0, count)]
            pltpu.make_async_copy(part, part, sem).wait()

    def send_b(step):
        send(b_ref, b_all.at[core, chip], b_sem, (chip_peer(step) * 2 + core, row))

    def send_b_across(step):
        there = chip_peer(step) * 2 + 1 - core
        send(b_ref, b_all.at[core, chip], cross_sem, (there, row))

    spread(1, chips, send_b)
    spread(0, chips, send_b_across)

    for load in loads[1:3]:
        load.wait()
    c_all[row] = c_ref[...]

    def send_c(step):
        there = lax.rem(row + step, narrow)
        send(c_ref, c_all.at[row], c_sem, (me, there))

    spread(1, narrow, send_c)
    fa = a_ref[...].astype(jnp.float32)
    eye = jnp.where(
        lax.broadcasted_iota(jnp.int32, (rank, rank), 0)
        == lax.broadcasted_iota(jnp.int32, (rank, rank), 1),
        1.0,
        0.0,
    )
    fc = nt(eye.astype(jnp.bfloat16), c_ref[...], None)
    a_rep = jnp.concatenate([fa] * k_local, axis=1)
    c_rep = jnp.concatenate(
        [jnp.broadcast_to(fc[:, k : k + 1], (rank, i_local)) for k in range(k_local)], axis=1
    )
    khatri = (a_rep * c_rep).astype(jnp.bfloat16)
    slots = (128 - 3 * rank) // 2
    lane_k = lax.broadcasted_iota(jnp.int32, (slots, k_local * i_local), 0)
    from_k = lax.broadcasted_iota(jnp.int32, (slots, k_local * i_local), 1) // i_local
    gather_k = jnp.where(lane_k == from_k + row * k_local, 1.0, 0.0)
    gram_a_own = nt(a_ref[...], a_ref[...], None) * jnp.where(row == 0, 1.0, 0.0)

    loads[3].wait()
    def columns(side):
        return jnp.concatenate(
            [
                t_ref[:, pl.ds(pl.multiple_of((at * 2 + side) * j_local, j_local), j_local)]
                for at in range(chips)
            ],
            axis=1,
        )

    def partial_b(side):
        part = jnp.dot(khatri, columns(side), preferred_element_type=jnp.float32)
        for at in range(chips):
            pb_send[side, at] = part[:, at * j_local : (at + 1) * j_local]

    partial_b(1 - core)
    send(pb_send.at[1 - core], pb_half, half_sem, partner)
    partial_b(core)

    def contract(side):
        blocks = jnp.concatenate([b_all[side, at] for at in range(chips)], axis=1)
        return nt(blocks, columns(side), None)

    settle(b_all.at[core], chips - 1, b_sem.at[1])
    contracted = contract(core)
    settle(pb_half, chips, half_sem.at[1])
    for at in range(chips):
        pb_half[at] = pb_half[at] + pb_send[core, at]

    def send_pb(step):
        there = chip_peer(step)
        send(pb_half.at[there], pb_all.at[chip], pb_sem, (there * 2 + core, row))

    spread(1, chips, send_pb)
    pb_all[chip] = pb_half[chip]
    settle(b_all.at[1 - core], chips, cross_sem.at[1])
    contracted = contracted + contract(1 - core)
    def packed(parts, column):
        head = column.astype(jnp.bfloat16).astype(jnp.float32)
        return jnp.concatenate(parts + [head, column - head], axis=1).astype(jnp.bfloat16)

    def summed_small(buffer):
        whole = jnp.sum(buffer[...].astype(jnp.float32), axis=0)
        at = 3 * rank
        return whole[:, :at], whole[:, at : at + slots] + whole[:, at + slots :]

    weighted = c_rep * contracted
    part_a = weighted[:, :i_local]
    for k in range(1, k_local):
        part_a = part_a + weighted[:, k * i_local : (k + 1) * i_local]
    pair_a = nt(a_rep, weighted)
    pair_b = nt(contracted, khatri.astype(jnp.float32))
    product = a_rep * contracted
    column_c = nt(product, gather_k)
    p_all[mine] = packed([pair_a, pair_b, gram_a_own], column_c)

    def send_p(step):
        send(p_all.at[mine], p_all.at[mine], p_sem, group_peer(step))

    spread(1, group, send_p)
    settle(c_all, narrow - 1, c_sem.at[1])
    whole_c = jnp.concatenate(
        [nt(eye.astype(jnp.bfloat16), c_all[n], None) for n in range(narrow)], axis=1
    )
    factor_b = jnp.concatenate([b_all[w % 2, w // 2] for w in range(wide)], axis=1)
    gram_b = nt(factor_b, factor_b, None)
    gram_c = nt(whole_c, whole_c)
    had_a = gram_b * gram_c
    settle(p_all, group - 1, p_sem.at[1])
    head, column = summed_small(p_all)
    w_all[layer] = packed([head], column)

    def send_w(step):
        send(w_all.at[layer], w_all.at[layer], w_sem, layer_peer(step))

    spread(1, high, send_w)

    settle(pb_all, chips - 1, pb_sem.at[1])
    part_b = jnp.sum(pb_all[...], axis=0)
    m_send[0] = part_b
    m_send[1, :, :i_local] = part_a
    m_all[row] = m_send[...]

    def send_m(step):
        there = lax.rem(row + step, narrow)
        send(m_send, m_all.at[row], m_sem, (me, there))

    spread(1, narrow, send_m)
    fb = b_ref[...].astype(jnp.float32)
    model_a = mm(had_a, fa)
    settle(m_all, narrow - 1, m_sem.at[1])
    summed = jnp.sum(m_all[...], axis=0)
    grad_a = summed[1][:, :i_local] - model_a
    had_grad_a = mm(had_a, grad_a)

    settle(w_all, high - 1, w_sem.at[1])
    small, column = summed_small(w_all)
    gram_a = small[:, 2 * rank : 3 * rank]
    mttkrp_c = column[:, :k_whole]
    had_b = gram_a * gram_c
    had_c = gram_a * gram_b
    cross_a = small[:, :rank] - mm(gram_a, had_a)
    cross_b = small[:, rank : 2 * rank] - mm(gram_b, had_b)
    cross_c = nt(whole_c, mttkrp_c) - mm(gram_c, had_c)
    grad_b = summed[0] - mm(had_b, fb)
    grad_c = mttkrp_c - mm(had_c, whole_c)
    mixed_a = cross_b * gram_c + gram_b * cross_c
    mixed_b = cross_a * gram_c + gram_a * cross_c
    mixed_c = cross_a * gram_b + gram_a * cross_b

    had_grad_b = mm(had_b, grad_b)
    had_grad_c = mm(had_c, grad_c)
    image_a = had_grad_a + mm(mixed_a, fa) + damping * grad_a
    image_b = had_grad_b + mm(mixed_b, fb) + damping * grad_b
    image_c = had_grad_c + mm(mixed_c, whole_c) + damping * grad_c
    sums = (
        total(grad_a * grad_a) + total(grad_b * grad_b),
        total(grad_a * had_grad_a) + total(grad_b * had_grad_b),
        total(image_a * image_a) + total(image_b * image_b),
        total(image_a * mm(had_a, image_a)) + total(image_b * mm(had_b, image_b)),
    )
    place = lax.broadcasted_iota(jnp.int32, (1, 128), 1)
    tile = jnp.zeros((1, 128), jnp.float32)
    for at, value in enumerate(sums):
        tile = jnp.where(place == at, value, tile)
    s_all[me] = tile

    def send_s(step):
        send(s_all.at[me], s_all.at[me], s_sem, (wide_peer(step), row))

    spread(1, wide, send_s)

    next_a = mm(cross_a, had_a) + damping * cross_a + nt(gram_a, mixed_a)
    next_b = mm(cross_b, had_b) + damping * cross_b + nt(gram_b, mixed_b)
    next_c = nt(whole_c, image_c)
    later_a = next_b * gram_c + gram_b * next_c
    later_b = next_a * gram_c + gram_a * next_c
    later_c = next_a * gram_b + gram_a * next_b
    known_gg = total(grad_c * grad_c)
    known_gh = total(grad_c * had_grad_c) + total(
        mixed_a * cross_a.T + mixed_b * cross_b.T + mixed_c * cross_c.T
    )
    known_qq = total(image_c * image_c)
    known_qh = total(image_c * mm(had_c, image_c)) + total(
        later_a * next_a.T + later_b * next_b.T + later_c * next_c.T
    )

    chosen = jnp.where(
        lax.broadcasted_iota(jnp.int32, (k_local, k_whole), 1)
        == lax.broadcasted_iota(jnp.int32, (k_local, k_whole), 0) + row * k_local,
        1.0,
        0.0,
    )
    own_grad_c, own_image_c = nt(chosen, grad_c), nt(chosen, image_c)

    settle(s_all, wide - 1, s_sem.at[1])
    tile = jnp.sum(s_all[...], axis=0)
    norm_0 = tile[:, 0:1] + known_gg
    curve_0 = tile[:, 1:2] + known_gh + damping * norm_0
    image_2 = tile[:, 2:3] + known_qq
    image_3 = tile[:, 3:4] + known_qh + damping * image_2

    alpha_0 = norm_0 / curve_0
    norm_1 = norm_0 - 2.0 * alpha_0 * curve_0 + alpha_0 * alpha_0 * image_2
    beta = norm_1 / norm_0
    gain = 1.0 + beta
    curve_1 = gain * gain * curve_0 - 2.0 * gain * alpha_0 * image_2 + alpha_0 * alpha_0 * image_3
    alpha_1 = norm_1 / curve_1
    on_grad = alpha_0 + alpha_1 * gain
    on_image = -alpha_1 * alpha_0
    out_a[...] = on_grad * grad_a + on_image * image_a
    out_b[...] = on_grad * grad_b + on_image * image_b
    out_c[...] = on_grad * own_grad_c + on_image * own_image_c

    settle(c_all, narrow - 1, c_sem.at[0])
    settle(b_all.at[0], chips - 1, b_sem.at[0])
    settle(b_all.at[0], chips, cross_sem.at[0])
    settle(pb_half, chips, half_sem.at[0])
    settle(pb_all, chips - 1, pb_sem.at[0])
    settle(p_all, group - 1, p_sem.at[0])
    settle(w_all, high - 1, w_sem.at[0])
    settle(m_all, narrow - 1, m_sem.at[0])
    settle(s_all, wide - 1, s_sem.at[0])


def write_out(in_a, in_b, in_c, out_a, out_b, out_c, sems):
    copies = [
        pltpu.make_async_copy(src, dst, sems.at[at])
        for at, (src, dst) in enumerate(((in_a, out_a), (in_b, out_b), (in_c, out_c)))
    ]
    for copy in copies:
        copy.start()
    for copy in copies:
        copy.wait()


def on_device(wide, narrow, tensor, factor_a, factor_b, factor_c):
    k_local, i_local, j_whole = tensor.shape
    rank, j_local = factor_b.shape
    flattened = tensor.reshape(k_local * i_local, j_whole)
    vmem = pl.BlockSpec(memory_space=pltpu.VMEM)
    anywhere = pl.BlockSpec(memory_space=pltpu.HBM)
    pair = pltpu.SemaphoreType.DMA((2,))
    f32, bf16 = jnp.float32, jnp.bfloat16
    chips = wide // 2
    low = 4 if wide % 4 == 0 else 2
    shapes = (
        jax.ShapeDtypeStruct((rank, i_local), f32),
        jax.ShapeDtypeStruct((rank, j_local), f32),
        jax.ShapeDtypeStruct((k_local, rank), f32),
    )
    steps = pl.pallas_call(
        functools.partial(kernel, wide, narrow, k_local),
        out_shape=shapes,
        in_specs=[anywhere] * 4,
        out_specs=(vmem, vmem, vmem),
        scratch_shapes=[
            pltpu.VMEM((k_local * i_local, j_whole), bf16),
            pltpu.VMEM((rank, i_local), bf16),
            pltpu.VMEM((rank, j_local), bf16),
            pltpu.VMEM((k_local, rank), bf16),
            pltpu.VMEM((narrow, k_local, rank), bf16),
            pltpu.VMEM((2, chips, rank, j_local), bf16),
            pltpu.VMEM((2, chips, rank, j_local), f32),
            pltpu.VMEM((chips, rank, j_local), f32),
            pltpu.VMEM((chips, rank, j_local), f32),
            pltpu.VMEM((low * narrow, rank, 128), bf16),
            pltpu.VMEM((wide // low, rank, 128), bf16),
            pltpu.VMEM((2, rank, 128), f32),
            pltpu.VMEM((narrow, 2, rank, 128), f32),
            pltpu.VMEM((wide, 1, 128), f32),
            pltpu.SemaphoreType.DMA((4,)),
            pair, pair, pair, pair, pair, pair, pair, pair, pair,
        ],
        compiler_params=pltpu.CompilerParams(collective_id=0, has_side_effects=True),
    )(flattened, factor_a, factor_b, factor_c.T)
    step_a, step_b, step_c = pl.pallas_call(
        write_out,
        out_shape=shapes,
        in_specs=[anywhere] * 3,
        out_specs=(anywhere,) * 3,
        scratch_shapes=[pltpu.SemaphoreType.DMA((3,))],
    )(*steps)
    return step_a, step_b, step_c.T


def solution(mesh):
    placed = (P("narrow", "wide", None), P(None, "wide"), P(None, "wide"), P(None, "narrow"))
    return jax.shard_map(
        functools.partial(on_device, mesh.shape["wide"], mesh.shape["narrow"]),
        mesh=mesh,
        in_specs=placed,
        out_specs=(P(None, "wide"), P(None, "wide"), P(None, "narrow")),
        check_vma=False,
    )
```

```python
import functools

import jax
import jax.numpy as jnp
from jax import lax
from jax.experimental import pallas as pl
from jax.experimental.pallas import tpu as pltpu
from jax.sharding import PartitionSpec as P

MESH = pl.DeviceIdType.MESH
highest = lax.Precision.HIGHEST
damping = 1.0


def mm(left, right):
    return jnp.dot(left, right, precision=highest, preferred_element_type=jnp.float32)


def nt(left, right, precision=highest):
    return lax.dot_general(
        left, right, (((1,), (1,)), ((), ())), precision=precision, preferred_element_type=jnp.float32
    )


def total(value):
    return jnp.sum(jnp.sum(value, axis=0, keepdims=True), axis=1, keepdims=True)


def spread(first, last, body):
    if last - first <= 3:
        for step in range(first, last):
            body(step)
        return

    def turn(step, carry):
        body(step)
        return carry

    lax.fori_loop(first, last, turn, 0)


def kernel(
    wide, narrow, k_local, t_hbm, a_hbm, b_hbm, c_hbm, out_a, out_b, out_c,
    t_ref, a_ref, b_ref, c_ref, c_all, b_all, pb_send, pb_half, pb_all, p_all, w_all,
    m_send, m_all, s_all,
    load_sem, c_sem, b_sem, cross_sem, half_sem, pb_sem, p_sem, w_sem, m_sem, s_sem,
):
    me = lax.axis_index("wide")
    row = lax.axis_index("narrow")
    core = lax.rem(me, 2)
    chip = me // 2
    chips = wide // 2
    low = 4 if wide % 4 == 0 else 2
    high = wide // low
    group = low * narrow
    layer, side_low = me // low, lax.rem(me, low)
    mine = row * low + side_low
    partner = (chip * 2 + 1 - core, row)
    rank, i_local = a_ref.shape
    j_local = b_ref.shape[1]
    k_whole = narrow * k_local

    loads = [
        pltpu.make_async_copy(src, dst, load_sem.at[at])
        for at, (src, dst) in enumerate(
            ((b_hbm, b_ref), (c_hbm, c_ref), (a_hbm, a_ref), (t_hbm, t_ref))
        )
    ]
    for load in loads:
        load.start()

    def wide_peer(step):
        return lax.rem(me + step, wide)

    def chip_peer(step):
        return lax.rem(chip + step, chips)

    def group_peer(step):
        other = lax.rem(mine + step, group)
        return layer * low + lax.rem(other, low), other // low

    def layer_peer(step):
        return lax.rem(layer + step, high) * low + side_low, row

    barrier = pltpu.get_barrier_semaphore()

    def greet(step):
        pl.semaphore_signal(barrier, inc=1, device_id=(wide_peer(step), row), device_id_type=MESH)

    def greet_row(step):
        there = lax.rem(row + step, narrow)
        for side in range(low):
            pl.semaphore_signal(
                barrier, inc=1, device_id=(layer * low + side, there), device_id_type=MESH
            )

    spread(1, wide, greet)
    spread(1, narrow, greet_row)
    loads[0].wait()
    b_all[core, chip] = b_ref[...]
    pl.semaphore_wait(barrier, (wide - 1) + low * (narrow - 1))

    def send(src, dst, sems, device):
        pltpu.make_async_remote_copy(
            src_ref=src, dst_ref=dst, send_sem=sems.at[0], recv_sem=sems.at[1],
            device_id=device, device_id_type=MESH,
        ).start()

    def settle(buffer, count, sem):
        if count > 0:
            part = buffer.at[pl.ds(0, count)]
            pltpu.make_async_copy(part, part, sem).wait()

    def send_b(step):
        send(b_ref, b_all.at[core, chip], b_sem, (chip_peer(step) * 2 + core, row))

    def send_b_across(step):
        there = chip_peer(step) * 2 + 1 - core
        send(b_ref, b_all.at[core, chip], cross_sem, (there, row))

    spread(1, chips, send_b)
    spread(0, chips, send_b_across)

    for load in loads[1:3]:
        load.wait()
    c_all[row] = c_ref[...]

    def send_c(step):
        there = lax.rem(row + step, narrow)
        send(c_ref, c_all.at[row], c_sem, (me, there))

    spread(1, narrow, send_c)
    fa = a_ref[...].astype(jnp.float32)
    eye = jnp.where(
        lax.broadcasted_iota(jnp.int32, (rank, rank), 0)
        == lax.broadcasted_iota(jnp.int32, (rank, rank), 1),
        1.0,
        0.0,
    )
    fc = nt(eye.astype(jnp.bfloat16), c_ref[...], None)
    a_rep = jnp.concatenate([fa] * k_local, axis=1)
    c_rep = jnp.concatenate(
        [jnp.broadcast_to(fc[:, k : k + 1], (rank, i_local)) for k in range(k_local)], axis=1
    )
    khatri = (a_rep * c_rep).astype(jnp.bfloat16)
    slots = (128 - 3 * rank) // 2
    lane_k = lax.broadcasted_iota(jnp.int32, (slots, k_local * i_local), 0)
    from_k = lax.broadcasted_iota(jnp.int32, (slots, k_local * i_local), 1) // i_local
    gather_k = jnp.where(lane_k == from_k + row * k_local, 1.0, 0.0)
    gram_a_own = nt(a_ref[...], a_ref[...], None) * jnp.where(row == 0, 1.0, 0.0)

    loads[3].wait()
    def columns(side):
        return jnp.concatenate(
            [
                t_ref[:, pl.ds(pl.multiple_of((at * 2 + side) * j_local, j_local), j_local)]
                for at in range(chips)
            ],
            axis=1,
        )

    def partial_b(side):
        part = jnp.dot(khatri, columns(side), preferred_element_type=jnp.float32)
        for at in range(chips):
            pb_send[side, at] = part[:, at * j_local : (at + 1) * j_local]

    partial_b(1 - core)
    send(pb_send.at[1 - core], pb_half, half_sem, partner)
    partial_b(core)

    def contract(side):
        blocks = jnp.concatenate([b_all[side, at] for at in range(chips)], axis=1)
        return nt(blocks, columns(side), None)

    settle(b_all.at[core], chips - 1, b_sem.at[1])
    contracted = contract(core)
    settle(pb_half, chips, half_sem.at[1])
    for at in range(chips):
        pb_half[at] = pb_half[at] + pb_send[core, at]

    def send_pb(step):
        there = chip_peer(step)
        send(pb_half.at[there], pb_all.at[chip], pb_sem, (there * 2 + core, row))

    spread(1, chips, send_pb)
    pb_all[chip] = pb_half[chip]
    settle(b_all.at[1 - core], chips, cross_sem.at[1])
    contracted = contracted + contract(1 - core)
    def packed(parts, column):
        head = column.astype(jnp.bfloat16).astype(jnp.float32)
        return jnp.concatenate(parts + [head, column - head], axis=1).astype(jnp.bfloat16)

    def summed_small(buffer):
        whole = jnp.sum(buffer[...].astype(jnp.float32), axis=0)
        at = 3 * rank
        return whole[:, :at], whole[:, at : at + slots] + whole[:, at + slots :]

    weighted = c_rep * contracted
    part_a = weighted[:, :i_local]
    for k in range(1, k_local):
        part_a = part_a + weighted[:, k * i_local : (k + 1) * i_local]
    pair_a = nt(a_rep.astype(jnp.bfloat16), weighted.astype(jnp.bfloat16), None)
    pair_b = nt(contracted.astype(jnp.bfloat16), khatri, None)
    product = a_rep * contracted
    column_c = nt(product, gather_k)
    p_all[mine] = packed([pair_a, pair_b, gram_a_own], column_c)

    def send_p(step):
        send(p_all.at[mine], p_all.at[mine], p_sem, group_peer(step))

    spread(1, group, send_p)
    settle(c_all, narrow - 1, c_sem.at[1])
    whole_c = jnp.concatenate(
        [nt(eye.astype(jnp.bfloat16), c_all[n], None) for n in range(narrow)], axis=1
    )
    factor_b = jnp.concatenate([b_all[w % 2, w // 2] for w in range(wide)], axis=1)
    gram_b = nt(factor_b, factor_b, None)
    gram_c = nt(whole_c, whole_c)
    had_a = gram_b * gram_c
    settle(p_all, group - 1, p_sem.at[1])
    head, column = summed_small(p_all)
    w_all[layer] = packed([head], column)

    def send_w(step):
        send(w_all.at[layer], w_all.at[layer], w_sem, layer_peer(step))

    spread(1, high, send_w)

    settle(pb_all, chips - 1, pb_sem.at[1])
    part_b = jnp.sum(pb_all[...], axis=0)
    m_send[0] = part_b
    m_send[1, :, :i_local] = part_a
    m_all[row] = m_send[...]

    def send_m(step):
        there = lax.rem(row + step, narrow)
        send(m_send, m_all.at[row], m_sem, (me, there))

    spread(1, narrow, send_m)
    fb = b_ref[...].astype(jnp.float32)
    model_a = mm(had_a, fa)
    settle(m_all, narrow - 1, m_sem.at[1])
    summed = jnp.sum(m_all[...], axis=0)
    grad_a = summed[1][:, :i_local] - model_a
    had_grad_a = mm(had_a, grad_a)

    settle(w_all, high - 1, w_sem.at[1])
    small, column = summed_small(w_all)
    gram_a = small[:, 2 * rank : 3 * rank]
    mttkrp_c = column[:, :k_whole]
    had_b = gram_a * gram_c
    had_c = gram_a * gram_b
    cross_a = small[:, :rank] - mm(gram_a, had_a)
    cross_b = small[:, rank : 2 * rank] - mm(gram_b, had_b)
    cross_c = nt(whole_c, mttkrp_c) - mm(gram_c, had_c)
    grad_b = summed[0] - mm(had_b, fb)
    grad_c = mttkrp_c - mm(had_c, whole_c)
    mixed_a = cross_b * gram_c + gram_b * cross_c
    mixed_b = cross_a * gram_c + gram_a * cross_c
    mixed_c = cross_a * gram_b + gram_a * cross_b

    had_grad_b = mm(had_b, grad_b)
    had_grad_c = mm(had_c, grad_c)
    image_a = had_grad_a + mm(mixed_a, fa) + damping * grad_a
    image_b = had_grad_b + mm(mixed_b, fb) + damping * grad_b
    image_c = had_grad_c + mm(mixed_c, whole_c) + damping * grad_c
    sums = (
        total(grad_a * grad_a) + total(grad_b * grad_b),
        total(grad_a * had_grad_a) + total(grad_b * had_grad_b),
        total(image_a * image_a) + total(image_b * image_b),
        total(image_a * mm(had_a, image_a)) + total(image_b * mm(had_b, image_b)),
    )
    place = lax.broadcasted_iota(jnp.int32, (1, 128), 1)
    tile = jnp.zeros((1, 128), jnp.float32)
    for at, value in enumerate(sums):
        tile = jnp.where(place == at, value, tile)
    s_all[me] = tile

    def send_s(step):
        send(s_all.at[me], s_all.at[me], s_sem, (wide_peer(step), row))

    spread(1, wide, send_s)

    next_a = mm(cross_a, had_a) + damping * cross_a + nt(gram_a, mixed_a)
    next_b = mm(cross_b, had_b) + damping * cross_b + nt(gram_b, mixed_b)
    next_c = nt(whole_c, image_c)
    later_a = next_b * gram_c + gram_b * next_c
    later_b = next_a * gram_c + gram_a * next_c
    later_c = next_a * gram_b + gram_a * next_b
    known_gg = total(grad_c * grad_c)
    known_gh = total(grad_c * had_grad_c) + total(
        mixed_a * cross_a.T + mixed_b * cross_b.T + mixed_c * cross_c.T
    )
    known_qq = total(image_c * image_c)
    known_qh = total(image_c * mm(had_c, image_c)) + total(
        later_a * next_a.T + later_b * next_b.T + later_c * next_c.T
    )

    chosen = jnp.where(
        lax.broadcasted_iota(jnp.int32, (k_local, k_whole), 1)
        == lax.broadcasted_iota(jnp.int32, (k_local, k_whole), 0) + row * k_local,
        1.0,
        0.0,
    )
    own_grad_c, own_image_c = nt(chosen, grad_c), nt(chosen, image_c)

    settle(s_all, wide - 1, s_sem.at[1])
    tile = jnp.sum(s_all[...], axis=0)
    norm_0 = tile[:, 0:1] + known_gg
    curve_0 = tile[:, 1:2] + known_gh + damping * norm_0
    image_2 = tile[:, 2:3] + known_qq
    image_3 = tile[:, 3:4] + known_qh + damping * image_2

    alpha_0 = norm_0 / curve_0
    norm_1 = norm_0 - 2.0 * alpha_0 * curve_0 + alpha_0 * alpha_0 * image_2
    beta = norm_1 / norm_0
    gain = 1.0 + beta
    curve_1 = gain * gain * curve_0 - 2.0 * gain * alpha_0 * image_2 + alpha_0 * alpha_0 * image_3
    alpha_1 = norm_1 / curve_1
    on_grad = alpha_0 + alpha_1 * gain
    on_image = -alpha_1 * alpha_0
    out_a[...] = on_grad * grad_a + on_image * image_a
    out_b[...] = on_grad * grad_b + on_image * image_b
    out_c[...] = on_grad * own_grad_c + on_image * own_image_c

    settle(c_all, narrow - 1, c_sem.at[0])
    settle(b_all.at[0], chips - 1, b_sem.at[0])
    settle(b_all.at[0], chips, cross_sem.at[0])
    settle(pb_half, chips, half_sem.at[0])
    settle(pb_all, chips - 1, pb_sem.at[0])
    settle(p_all, group - 1, p_sem.at[0])
    settle(w_all, high - 1, w_sem.at[0])
    settle(m_all, narrow - 1, m_sem.at[0])
    settle(s_all, wide - 1, s_sem.at[0])


def write_out(in_a, in_b, in_c, out_a, out_b, out_c, sems):
    copies = [
        pltpu.make_async_copy(src, dst, sems.at[at])
        for at, (src, dst) in enumerate(((in_a, out_a), (in_b, out_b), (in_c, out_c)))
    ]
    for copy in copies:
        copy.start()
    for copy in copies:
        copy.wait()


def on_device(wide, narrow, tensor, factor_a, factor_b, factor_c):
    k_local, i_local, j_whole = tensor.shape
    rank, j_local = factor_b.shape
    flattened = tensor.reshape(k_local * i_local, j_whole)
    vmem = pl.BlockSpec(memory_space=pltpu.VMEM)
    anywhere = pl.BlockSpec(memory_space=pltpu.HBM)
    pair = pltpu.SemaphoreType.DMA((2,))
    f32, bf16 = jnp.float32, jnp.bfloat16
    chips = wide // 2
    low = 4 if wide % 4 == 0 else 2
    shapes = (
        jax.ShapeDtypeStruct((rank, i_local), f32),
        jax.ShapeDtypeStruct((rank, j_local), f32),
        jax.ShapeDtypeStruct((k_local, rank), f32),
    )
    steps = pl.pallas_call(
        functools.partial(kernel, wide, narrow, k_local),
        out_shape=shapes,
        in_specs=[anywhere] * 4,
        out_specs=(vmem, vmem, vmem),
        scratch_shapes=[
            pltpu.VMEM((k_local * i_local, j_whole), bf16),
            pltpu.VMEM((rank, i_local), bf16),
            pltpu.VMEM((rank, j_local), bf16),
            pltpu.VMEM((k_local, rank), bf16),
            pltpu.VMEM((narrow, k_local, rank), bf16),
            pltpu.VMEM((2, chips, rank, j_local), bf16),
            pltpu.VMEM((2, chips, rank, j_local), f32),
            pltpu.VMEM((chips, rank, j_local), f32),
            pltpu.VMEM((chips, rank, j_local), f32),
            pltpu.VMEM((low * narrow, rank, 128), bf16),
            pltpu.VMEM((wide // low, rank, 128), bf16),
            pltpu.VMEM((2, rank, 128), f32),
            pltpu.VMEM((narrow, 2, rank, 128), f32),
            pltpu.VMEM((wide, 1, 128), f32),
            pltpu.SemaphoreType.DMA((4,)),
            pair, pair, pair, pair, pair, pair, pair, pair, pair,
        ],
        compiler_params=pltpu.CompilerParams(collective_id=0, has_side_effects=True),
    )(flattened, factor_a, factor_b, factor_c.T)
    step_a, step_b, step_c = pl.pallas_call(
        write_out,
        out_shape=shapes,
        in_specs=[anywhere] * 3,
        out_specs=(anywhere,) * 3,
        scratch_shapes=[pltpu.SemaphoreType.DMA((3,))],
    )(*steps)
    return step_a, step_b, step_c.T


def solution(mesh):
    placed = (P("narrow", "wide", None), P(None, "wide"), P(None, "wide"), P(None, "narrow"))
    return jax.shard_map(
        functools.partial(on_device, mesh.shape["wide"], mesh.shape["narrow"]),
        mesh=mesh,
        in_specs=placed,
        out_specs=(P(None, "wide"), P(None, "wide"), P(None, "narrow")),
        check_vma=False,
    )
```

```python
import functools

import jax
import jax.numpy as jnp
from jax import lax
from jax.experimental import pallas as pl
from jax.experimental.pallas import tpu as pltpu
from jax.sharding import PartitionSpec as P

MESH = pl.DeviceIdType.MESH
damping = 1.0


def halves(value):
    if value.dtype == jnp.bfloat16:
        return (value,)
    high = value.astype(jnp.bfloat16)
    return high, (value - high.astype(jnp.float32)).astype(jnp.bfloat16)


def contract_by(left, right, dims):
    out = None
    for at, one in enumerate(halves(left)):
        for to, other in enumerate(halves(right)):
            if at + to < 2:
                term = lax.dot_general(
                    one, other, (dims, ((), ())), preferred_element_type=jnp.float32
                )
                out = term if out is None else out + term
    return out


def mm(left, right):
    return contract_by(left, right, ((1,), (0,)))


def nt(left, right):
    return contract_by(left, right, ((1,), (1,)))


def total(value):
    return jnp.sum(jnp.sum(value, axis=0, keepdims=True), axis=1, keepdims=True)


def spread(first, last, body):
    if last - first <= 3:
        for step in range(first, last):
            body(step)
        return

    def turn(step, carry):
        body(step)
        return carry

    lax.fori_loop(first, last, turn, 0)


def kernel(
    wide, narrow, k_local, t_hbm, a_hbm, b_hbm, c_hbm, out_a, out_b, out_c,
    t_ref, a_ref, b_ref, c_ref, c_all, b_all, pb_send, pb_half, pb_all, p_all, w_all,
    m_send, m_all, s_all,
    load_sem, c_sem, b_sem, cross_sem, half_sem, pb_sem, p_sem, w_sem, m_sem, s_sem,
):
    me = lax.axis_index("wide")
    row = lax.axis_index("narrow")
    core = lax.rem(me, 2)
    chip = me // 2
    chips = wide // 2
    low = 4 if wide % 4 == 0 else 2
    high = wide // low
    group = low * narrow
    layer, side_low = me // low, lax.rem(me, low)
    mine = row * low + side_low
    partner = (chip * 2 + 1 - core, row)
    rank, i_local = a_ref.shape
    j_local = b_ref.shape[1]
    k_whole = narrow * k_local

    loads = [
        pltpu.make_async_copy(src, dst, load_sem.at[at])
        for at, (src, dst) in enumerate(
            ((b_hbm, b_ref), (c_hbm, c_ref), (a_hbm, a_ref), (t_hbm, t_ref))
        )
    ]
    for load in loads:
        load.start()

    def wide_peer(step):
        return lax.rem(me + step, wide)

    def chip_peer(step):
        return lax.rem(chip + step, chips)

    def group_peer(step):
        other = lax.rem(mine + step, group)
        return layer * low + lax.rem(other, low), other // low

    def layer_peer(step):
        return lax.rem(layer + step, high) * low + side_low, row

    barrier = pltpu.get_barrier_semaphore()

    def greet(step):
        pl.semaphore_signal(barrier, inc=1, device_id=(wide_peer(step), row), device_id_type=MESH)

    def greet_row(step):
        there = lax.rem(row + step, narrow)
        for side in range(low):
            pl.semaphore_signal(
                barrier, inc=1, device_id=(layer * low + side, there), device_id_type=MESH
            )

    spread(1, wide, greet)
    spread(1, narrow, greet_row)
    loads[0].wait()
    b_all[core, chip] = b_ref[...]
    pl.semaphore_wait(barrier, (wide - 1) + low * (narrow - 1))

    def send(src, dst, sems, device):
        pltpu.make_async_remote_copy(
            src_ref=src, dst_ref=dst, send_sem=sems.at[0], recv_sem=sems.at[1],
            device_id=device, device_id_type=MESH,
        ).start()

    def settle(buffer, count, sem):
        if count > 0:
            part = buffer.at[pl.ds(0, count)]
            pltpu.make_async_copy(part, part, sem).wait()

    def send_b(step):
        send(b_ref, b_all.at[core, chip], b_sem, (chip_peer(step) * 2 + core, row))

    def send_b_across(step):
        there = chip_peer(step) * 2 + 1 - core
        send(b_ref, b_all.at[core, chip], cross_sem, (there, row))

    spread(1, chips, send_b)
    spread(0, chips, send_b_across)

    for load in loads[1:3]:
        load.wait()
    c_all[row] = c_ref[...]

    def send_c(step):
        there = lax.rem(row + step, narrow)
        send(c_ref, c_all.at[row], c_sem, (me, there))

    spread(1, narrow, send_c)
    fa = a_ref[...].astype(jnp.float32)
    eye = jnp.where(
        lax.broadcasted_iota(jnp.int32, (rank, rank), 0)
        == lax.broadcasted_iota(jnp.int32, (rank, rank), 1),
        1.0,
        0.0,
    ).astype(jnp.bfloat16)
    fc = nt(eye, c_ref[...])
    a_rep = jnp.concatenate([fa] * k_local, axis=1)
    c_rep = jnp.concatenate(
        [jnp.broadcast_to(fc[:, k : k + 1], (rank, i_local)) for k in range(k_local)], axis=1
    )
    khatri = (a_rep * c_rep).astype(jnp.bfloat16)
    slots = (128 - 3 * rank) // 2
    lane_k = lax.broadcasted_iota(jnp.int32, (slots, k_local * i_local), 0)
    from_k = lax.broadcasted_iota(jnp.int32, (slots, k_local * i_local), 1) // i_local
    gather_k = jnp.where(lane_k == from_k + row * k_local, 1.0, 0.0).astype(jnp.bfloat16)
    gram_a_own = nt(a_ref[...], a_ref[...]) * jnp.where(row == 0, 1.0, 0.0)

    loads[3].wait()
    def columns(side):
        return jnp.concatenate(
            [
                t_ref[:, pl.ds(pl.multiple_of((at * 2 + side) * j_local, j_local), j_local)]
                for at in range(chips)
            ],
            axis=1,
        )

    def partial_b(side):
        part = jnp.dot(khatri, columns(side), preferred_element_type=jnp.float32)
        for at in range(chips):
            pb_send[side, at] = part[:, at * j_local : (at + 1) * j_local]

    partial_b(1 - core)
    send(pb_send.at[1 - core], pb_half, half_sem, partner)
    partial_b(core)

    def contract(side):
        blocks = jnp.concatenate([b_all[side, at] for at in range(chips)], axis=1)
        return nt(blocks, columns(side))

    settle(b_all.at[core], chips - 1, b_sem.at[1])
    contracted = contract(core)
    settle(pb_half, chips, half_sem.at[1])
    for at in range(chips):
        pb_half[at] = pb_half[at] + pb_send[core, at]

    def send_pb(step):
        there = chip_peer(step)
        send(pb_half.at[there], pb_all.at[chip], pb_sem, (there * 2 + core, row))

    spread(1, chips, send_pb)
    pb_all[chip] = pb_half[chip]
    settle(b_all.at[1 - core], chips, cross_sem.at[1])
    contracted = contracted + contract(1 - core)
    def packed(parts, column):
        head = column.astype(jnp.bfloat16).astype(jnp.float32)
        return jnp.concatenate(parts + [head, column - head], axis=1).astype(jnp.bfloat16)

    def summed_small(buffer):
        whole = jnp.sum(buffer[...].astype(jnp.float32), axis=0)
        at = 3 * rank
        return whole[:, :at], whole[:, at : at + slots] + whole[:, at + slots :]

    weighted = c_rep * contracted
    part_a = weighted[:, :i_local]
    for k in range(1, k_local):
        part_a = part_a + weighted[:, k * i_local : (k + 1) * i_local]
    pair_a = nt(a_rep.astype(jnp.bfloat16), weighted.astype(jnp.bfloat16))
    pair_b = nt(contracted.astype(jnp.bfloat16), khatri)
    product = a_rep * contracted
    column_c = nt(product, gather_k)
    p_all[mine] = packed([pair_a, pair_b, gram_a_own], column_c)

    def send_p(step):
        send(p_all.at[mine], p_all.at[mine], p_sem, group_peer(step))

    spread(1, group, send_p)
    settle(c_all, narrow - 1, c_sem.at[1])
    whole_c = jnp.concatenate(
        [nt(eye, c_all[n]).astype(jnp.bfloat16) for n in range(narrow)], axis=1
    )
    factor_b = jnp.concatenate([b_all[w % 2, w // 2] for w in range(wide)], axis=1)
    gram_b = nt(factor_b, factor_b)
    gram_c = nt(whole_c, whole_c)
    had_a = gram_b * gram_c
    settle(p_all, group - 1, p_sem.at[1])
    head, column = summed_small(p_all)
    w_all[layer] = packed([head], column)

    def send_w(step):
        send(w_all.at[layer], w_all.at[layer], w_sem, layer_peer(step))

    spread(1, high, send_w)

    settle(pb_all, chips - 1, pb_sem.at[1])
    part_b = jnp.sum(pb_all[...], axis=0)
    m_send[0] = part_b
    m_send[1, :, :i_local] = part_a
    m_all[row] = m_send[...]

    def send_m(step):
        there = lax.rem(row + step, narrow)
        send(m_send, m_all.at[row], m_sem, (me, there))

    spread(1, narrow, send_m)
    fa, fb = a_ref[...], b_ref[...]
    model_a = mm(had_a, fa)
    settle(m_all, narrow - 1, m_sem.at[1])
    summed = jnp.sum(m_all[...], axis=0)
    grad_a = summed[1][:, :i_local] - model_a
    had_grad_a = mm(had_a, grad_a)

    settle(w_all, high - 1, w_sem.at[1])
    small, column = summed_small(w_all)
    gram_a = small[:, 2 * rank : 3 * rank]
    mttkrp_c = column[:, :k_whole]
    had_b = gram_a * gram_c
    had_c = gram_a * gram_b
    cross_a = small[:, :rank] - mm(gram_a, had_a)
    cross_b = small[:, rank : 2 * rank] - mm(gram_b, had_b)
    cross_c = nt(whole_c, mttkrp_c) - mm(gram_c, had_c)
    grad_b = summed[0] - mm(had_b, fb)
    grad_c = mttkrp_c - mm(had_c, whole_c)
    mixed_a = cross_b * gram_c + gram_b * cross_c
    mixed_b = cross_a * gram_c + gram_a * cross_c
    mixed_c = cross_a * gram_b + gram_a * cross_b

    had_grad_b = mm(had_b, grad_b)
    had_grad_c = mm(had_c, grad_c)
    image_a = had_grad_a + mm(mixed_a, fa) + damping * grad_a
    image_b = had_grad_b + mm(mixed_b, fb) + damping * grad_b
    image_c = had_grad_c + mm(mixed_c, whole_c) + damping * grad_c
    sums = (
        total(grad_a * grad_a) + total(grad_b * grad_b),
        total(grad_a * had_grad_a) + total(grad_b * had_grad_b),
        total(image_a * image_a) + total(image_b * image_b),
        total(image_a * mm(had_a, image_a)) + total(image_b * mm(had_b, image_b)),
    )
    place = lax.broadcasted_iota(jnp.int32, (1, 128), 1)
    tile = jnp.zeros((1, 128), jnp.float32)
    for at, value in enumerate(sums):
        tile = jnp.where(place == at, value, tile)
    s_all[me] = tile

    def send_s(step):
        send(s_all.at[me], s_all.at[me], s_sem, (wide_peer(step), row))

    spread(1, wide, send_s)

    next_a = mm(cross_a, had_a) + damping * cross_a + nt(gram_a, mixed_a)
    next_b = mm(cross_b, had_b) + damping * cross_b + nt(gram_b, mixed_b)
    next_c = nt(whole_c, image_c)
    def paired(of_a, of_b, of_c):
        return 2.0 * total(
            of_a.T * (gram_c * of_b + gram_b * of_c) + gram_a * of_b.T * of_c
        )

    known_gg = total(grad_c * grad_c)
    known_gh = total(grad_c * had_grad_c) + paired(cross_a, cross_b, cross_c)
    known_qq = total(image_c * image_c)
    known_qh = total(image_c * mm(had_c, image_c)) + paired(next_a, next_b, next_c)

    chosen = jnp.where(
        lax.broadcasted_iota(jnp.int32, (k_local, k_whole), 1)
        == lax.broadcasted_iota(jnp.int32, (k_local, k_whole), 0) + row * k_local,
        1.0,
        0.0,
    ).astype(jnp.bfloat16)
    own_grad_c, own_image_c = nt(chosen, grad_c), nt(chosen, image_c)

    settle(s_all, wide - 1, s_sem.at[1])
    tile = jnp.sum(s_all[...], axis=0)
    norm_0 = tile[:, 0:1] + known_gg
    curve_0 = tile[:, 1:2] + known_gh + damping * norm_0
    image_2 = tile[:, 2:3] + known_qq
    image_3 = tile[:, 3:4] + known_qh + damping * image_2

    alpha_0 = norm_0 / curve_0
    norm_1 = norm_0 - 2.0 * alpha_0 * curve_0 + alpha_0 * alpha_0 * image_2
    beta = norm_1 / norm_0
    gain = 1.0 + beta
    curve_1 = gain * gain * curve_0 - 2.0 * gain * alpha_0 * image_2 + alpha_0 * alpha_0 * image_3
    alpha_1 = norm_1 / curve_1
    on_grad = alpha_0 + alpha_1 * gain
    on_image = -alpha_1 * alpha_0
    out_a[...] = on_grad * grad_a + on_image * image_a
    out_b[...] = on_grad * grad_b + on_image * image_b
    out_c[...] = on_grad * own_grad_c + on_image * own_image_c

    settle(c_all, narrow - 1, c_sem.at[0])
    settle(b_all.at[0], chips - 1, b_sem.at[0])
    settle(b_all.at[0], chips, cross_sem.at[0])
    settle(pb_half, chips, half_sem.at[0])
    settle(pb_all, chips - 1, pb_sem.at[0])
    settle(p_all, group - 1, p_sem.at[0])
    settle(w_all, high - 1, w_sem.at[0])
    settle(m_all, narrow - 1, m_sem.at[0])
    settle(s_all, wide - 1, s_sem.at[0])


def write_out(in_a, in_b, in_c, out_a, out_b, out_c, sems):
    copies = [
        pltpu.make_async_copy(src, dst, sems.at[at])
        for at, (src, dst) in enumerate(((in_a, out_a), (in_b, out_b), (in_c, out_c)))
    ]
    for copy in copies:
        copy.start()
    for copy in copies:
        copy.wait()


def on_device(wide, narrow, tensor, factor_a, factor_b, factor_c):
    k_local, i_local, j_whole = tensor.shape
    rank, j_local = factor_b.shape
    flattened = tensor.reshape(k_local * i_local, j_whole)
    vmem = pl.BlockSpec(memory_space=pltpu.VMEM)
    anywhere = pl.BlockSpec(memory_space=pltpu.HBM)
    pair = pltpu.SemaphoreType.DMA((2,))
    f32, bf16 = jnp.float32, jnp.bfloat16
    chips = wide // 2
    low = 4 if wide % 4 == 0 else 2
    shapes = (
        jax.ShapeDtypeStruct((rank, i_local), f32),
        jax.ShapeDtypeStruct((rank, j_local), f32),
        jax.ShapeDtypeStruct((k_local, rank), f32),
    )
    steps = pl.pallas_call(
        functools.partial(kernel, wide, narrow, k_local),
        out_shape=shapes,
        in_specs=[anywhere] * 4,
        out_specs=(vmem, vmem, vmem),
        scratch_shapes=[
            pltpu.VMEM((k_local * i_local, j_whole), bf16),
            pltpu.VMEM((rank, i_local), bf16),
            pltpu.VMEM((rank, j_local), bf16),
            pltpu.VMEM((k_local, rank), bf16),
            pltpu.VMEM((narrow, k_local, rank), bf16),
            pltpu.VMEM((2, chips, rank, j_local), bf16),
            pltpu.VMEM((2, chips, rank, j_local), f32),
            pltpu.VMEM((chips, rank, j_local), f32),
            pltpu.VMEM((chips, rank, j_local), f32),
            pltpu.VMEM((low * narrow, rank, 128), bf16),
            pltpu.VMEM((wide // low, rank, 128), bf16),
            pltpu.VMEM((2, rank, 128), f32),
            pltpu.VMEM((narrow, 2, rank, 128), f32),
            pltpu.VMEM((wide, 1, 128), f32),
            pltpu.SemaphoreType.DMA((4,)),
            pair, pair, pair, pair, pair, pair, pair, pair, pair,
        ],
        compiler_params=pltpu.CompilerParams(collective_id=0, has_side_effects=True),
    )(flattened, factor_a, factor_b, factor_c.T)
    step_a, step_b, step_c = pl.pallas_call(
        write_out,
        out_shape=shapes,
        in_specs=[anywhere] * 3,
        out_specs=(anywhere,) * 3,
        scratch_shapes=[pltpu.SemaphoreType.DMA((3,))],
    )(*steps)
    return step_a, step_b, step_c.T


def solution(mesh):
    placed = (P("narrow", "wide"), P(None, "wide"), P(None, "wide"), P(None, "narrow"))
    return jax.shard_map(
        functools.partial(on_device, mesh.shape["wide"], mesh.shape["narrow"]),
        mesh=mesh,
        in_specs=placed,
        out_specs=(P(None, "wide"), P(None, "wide"), P(None, "narrow")),
        check_vma=False,
    )
```

```python
import functools

import jax
import jax.numpy as jnp
from jax import lax
from jax.experimental import pallas as pl
from jax.experimental.pallas import tpu as pltpu
from jax.sharding import PartitionSpec as P

MESH = pl.DeviceIdType.MESH
damping = 1.0


def halves(value):
    if value.dtype == jnp.bfloat16:
        return (value,)
    high = value.astype(jnp.bfloat16)
    return high, (value - high.astype(jnp.float32)).astype(jnp.bfloat16)


def contract_by(left, right, dims):
    out = None
    for at, one in enumerate(halves(left)):
        for to, other in enumerate(halves(right)):
            if at + to < 2:
                term = lax.dot_general(
                    one, other, (dims, ((), ())), preferred_element_type=jnp.float32
                )
                out = term if out is None else out + term
    return out


def mm(left, right):
    return contract_by(left, right, ((1,), (0,)))


def nt(left, right):
    return contract_by(left, right, ((1,), (1,)))


def total(value):
    return jnp.sum(jnp.sum(value, axis=0, keepdims=True), axis=1, keepdims=True)


def spread(first, last, body):
    if last - first <= 3:
        for step in range(first, last):
            body(step)
        return

    def turn(step, carry):
        body(step)
        return carry

    lax.fori_loop(first, last, turn, 0)


def kernel(
    wide, narrow, k_local, t_hbm, a_hbm, b_hbm, c_hbm, a_out, b_out, c_out,
    out_a, out_b, out_c,
    t_ref, a_ref, b_ref, c_ref, c_all, b_all, pb_send, pb_half, pb_all, p_all, w_all,
    m_send, m_all, s_all,
    load_sem, out_sem, c_sem, b_sem, cross_sem, half_sem, pb_sem, p_sem, w_sem, m_sem, s_sem,
):
    me = lax.axis_index("wide")
    row = lax.axis_index("narrow")
    core = lax.rem(me, 2)
    chip = me // 2
    chips = wide // 2
    low = 4 if wide % 4 == 0 else 2
    high = wide // low
    group = low * narrow
    layer, side_low = me // low, lax.rem(me, low)
    mine = row * low + side_low
    partner = (chip * 2 + 1 - core, row)
    rank, i_local = a_ref.shape
    j_local = b_ref.shape[1]
    k_whole = narrow * k_local

    loads = [
        pltpu.make_async_copy(src, dst, load_sem.at[at])
        for at, (src, dst) in enumerate(
            ((b_hbm, b_ref), (c_hbm, c_ref), (a_hbm, a_ref), (t_hbm, t_ref))
        )
    ]
    for load in loads:
        load.start()

    def wide_peer(step):
        return lax.rem(me + step, wide)

    def chip_peer(step):
        return lax.rem(chip + step, chips)

    def group_peer(step):
        other = lax.rem(mine + step, group)
        return layer * low + lax.rem(other, low), other // low

    def layer_peer(step):
        return lax.rem(layer + step, high) * low + side_low, row

    barrier = pltpu.get_barrier_semaphore()

    def greet(step):
        pl.semaphore_signal(barrier, inc=1, device_id=(wide_peer(step), row), device_id_type=MESH)

    def greet_row(step):
        there = lax.rem(row + step, narrow)
        for side in range(low):
            pl.semaphore_signal(
                barrier, inc=1, device_id=(layer * low + side, there), device_id_type=MESH
            )

    spread(1, wide, greet)
    spread(1, narrow, greet_row)
    loads[0].wait()
    b_all[core, chip] = b_ref[...]
    pl.semaphore_wait(barrier, (wide - 1) + low * (narrow - 1))

    def send(src, dst, sems, device):
        pltpu.make_async_remote_copy(
            src_ref=src, dst_ref=dst, send_sem=sems.at[0], recv_sem=sems.at[1],
            device_id=device, device_id_type=MESH,
        ).start()

    def settle(buffer, count, sem):
        if count > 0:
            part = buffer.at[pl.ds(0, count)]
            pltpu.make_async_copy(part, part, sem).wait()

    def send_b(step):
        send(b_ref, b_all.at[core, chip], b_sem, (chip_peer(step) * 2 + core, row))

    def send_b_across(step):
        there = chip_peer(step) * 2 + 1 - core
        send(b_ref, b_all.at[core, chip], cross_sem, (there, row))

    spread(1, chips, send_b)
    spread(0, chips, send_b_across)

    for load in loads[1:3]:
        load.wait()
    c_all[row] = c_ref[...]

    def send_c(step):
        there = lax.rem(row + step, narrow)
        send(c_ref, c_all.at[row], c_sem, (me, there))

    spread(1, narrow, send_c)
    fa = a_ref[...].astype(jnp.float32)
    eye = jnp.where(
        lax.broadcasted_iota(jnp.int32, (rank, rank), 0)
        == lax.broadcasted_iota(jnp.int32, (rank, rank), 1),
        1.0,
        0.0,
    ).astype(jnp.bfloat16)
    fc = nt(eye, c_ref[...])
    a_rep = jnp.concatenate([fa] * k_local, axis=1)
    c_rep = jnp.concatenate(
        [jnp.broadcast_to(fc[:, k : k + 1], (rank, i_local)) for k in range(k_local)], axis=1
    )
    khatri = (a_rep * c_rep).astype(jnp.bfloat16)
    slots = (128 - 3 * rank) // 2
    lane_k = lax.broadcasted_iota(jnp.int32, (slots, k_local * i_local), 0)
    from_k = lax.broadcasted_iota(jnp.int32, (slots, k_local * i_local), 1) // i_local
    gather_k = jnp.where(lane_k == from_k + row * k_local, 1.0, 0.0).astype(jnp.bfloat16)
    gram_a_own = nt(a_ref[...], a_ref[...]) * jnp.where(row == 0, 1.0, 0.0)

    loads[3].wait()
    def columns(side):
        return jnp.concatenate(
            [
                t_ref[:, pl.ds(pl.multiple_of((at * 2 + side) * j_local, j_local), j_local)]
                for at in range(chips)
            ],
            axis=1,
        )

    def partial_b(side):
        part = jnp.dot(khatri, columns(side), preferred_element_type=jnp.float32)
        for at in range(chips):
            pb_send[side, at] = part[:, at * j_local : (at + 1) * j_local]

    partial_b(1 - core)
    send(pb_send.at[1 - core], pb_half, half_sem, partner)
    partial_b(core)

    def contract(side):
        blocks = jnp.concatenate([b_all[side, at] for at in range(chips)], axis=1)
        return nt(blocks, columns(side))

    settle(b_all.at[core], chips - 1, b_sem.at[1])
    contracted = contract(core)
    settle(pb_half, chips, half_sem.at[1])
    for at in range(chips):
        pb_half[at] = pb_half[at] + pb_send[core, at]

    def send_pb(step):
        there = chip_peer(step)
        send(pb_half.at[there], pb_all.at[chip], pb_sem, (there * 2 + core, row))

    spread(1, chips, send_pb)
    pb_all[chip] = pb_half[chip]
    settle(b_all.at[1 - core], chips, cross_sem.at[1])
    contracted = contracted + contract(1 - core)
    def packed(parts, column):
        head = column.astype(jnp.bfloat16).astype(jnp.float32)
        return jnp.concatenate(parts + [head, column - head], axis=1).astype(jnp.bfloat16)

    def summed_small(buffer):
        whole = jnp.sum(buffer[...].astype(jnp.float32), axis=0)
        at = 3 * rank
        return whole[:, :at], whole[:, at : at + slots] + whole[:, at + slots :]

    weighted = c_rep * contracted
    part_a = weighted[:, :i_local]
    for k in range(1, k_local):
        part_a = part_a + weighted[:, k * i_local : (k + 1) * i_local]
    pair_a = nt(a_rep.astype(jnp.bfloat16), weighted.astype(jnp.bfloat16))
    pair_b = nt(contracted.astype(jnp.bfloat16), khatri)
    product = a_rep * contracted
    column_c = nt(product, gather_k)
    p_all[mine] = packed([pair_a, pair_b, gram_a_own], column_c)

    def send_p(step):
        send(p_all.at[mine], p_all.at[mine], p_sem, group_peer(step))

    spread(1, group, send_p)
    settle(c_all, narrow - 1, c_sem.at[1])
    whole_c = jnp.concatenate(
        [nt(eye, c_all[n]).astype(jnp.bfloat16) for n in range(narrow)], axis=1
    )
    factor_b = jnp.concatenate([b_all[w % 2, w // 2] for w in range(wide)], axis=1)
    gram_b = nt(factor_b, factor_b)
    gram_c = nt(whole_c, whole_c)
    had_a = gram_b * gram_c
    settle(p_all, group - 1, p_sem.at[1])
    head, column = summed_small(p_all)
    w_all[layer] = packed([head], column)

    def send_w(step):
        send(w_all.at[layer], w_all.at[layer], w_sem, layer_peer(step))

    spread(1, high, send_w)

    settle(pb_all, chips - 1, pb_sem.at[1])
    part_b = jnp.sum(pb_all[...], axis=0)
    m_send[0] = part_b
    m_send[1, :, :i_local] = part_a
    m_all[row] = m_send[...]

    def send_m(step):
        there = lax.rem(row + step, narrow)
        send(m_send, m_all.at[row], m_sem, (me, there))

    spread(1, narrow, send_m)
    fa, fb = a_ref[...], b_ref[...]
    model_a = mm(had_a, fa)
    settle(m_all, narrow - 1, m_sem.at[1])
    summed = jnp.sum(m_all[...], axis=0)
    grad_a = summed[1][:, :i_local] - model_a
    had_grad_a = mm(had_a, grad_a)

    settle(w_all, high - 1, w_sem.at[1])
    small, column = summed_small(w_all)
    gram_a = small[:, 2 * rank : 3 * rank]
    mttkrp_c = column[:, :k_whole]
    had_b = gram_a * gram_c
    had_c = gram_a * gram_b
    cross_a = small[:, :rank] - mm(gram_a, had_a)
    cross_b = small[:, rank : 2 * rank] - mm(gram_b, had_b)
    cross_c = nt(whole_c, mttkrp_c) - mm(gram_c, had_c)
    grad_b = summed[0] - mm(had_b, fb)
    grad_c = mttkrp_c - mm(had_c, whole_c)
    mixed_a = cross_b * gram_c + gram_b * cross_c
    mixed_b = cross_a * gram_c + gram_a * cross_c
    mixed_c = cross_a * gram_b + gram_a * cross_b

    had_grad_b = mm(had_b, grad_b)
    had_grad_c = mm(had_c, grad_c)
    image_a = had_grad_a + mm(mixed_a, fa) + damping * grad_a
    image_b = had_grad_b + mm(mixed_b, fb) + damping * grad_b
    image_c = had_grad_c + mm(mixed_c, whole_c) + damping * grad_c
    sums = (
        total(grad_a * grad_a) + total(grad_b * grad_b),
        total(grad_a * had_grad_a) + total(grad_b * had_grad_b),
        total(image_a * image_a) + total(image_b * image_b),
        total(image_a * mm(had_a, image_a)) + total(image_b * mm(had_b, image_b)),
    )
    place = lax.broadcasted_iota(jnp.int32, (1, 128), 1)
    tile = jnp.zeros((1, 128), jnp.float32)
    for at, value in enumerate(sums):
        tile = jnp.where(place == at, value, tile)
    s_all[me] = tile

    def send_s(step):
        send(s_all.at[me], s_all.at[me], s_sem, (wide_peer(step), row))

    spread(1, wide, send_s)

    next_a = mm(cross_a, had_a) + damping * cross_a + nt(gram_a, mixed_a)
    next_b = mm(cross_b, had_b) + damping * cross_b + nt(gram_b, mixed_b)
    next_c = nt(whole_c, image_c)
    def paired(of_a, of_b, of_c):
        return 2.0 * total(
            of_a.T * (gram_c * of_b + gram_b * of_c) + gram_a * of_b.T * of_c
        )

    known_gg = total(grad_c * grad_c)
    known_gh = total(grad_c * had_grad_c) + paired(cross_a, cross_b, cross_c)
    known_qq = total(image_c * image_c)
    known_qh = total(image_c * mm(had_c, image_c)) + paired(next_a, next_b, next_c)

    chosen = jnp.where(
        lax.broadcasted_iota(jnp.int32, (k_local, k_whole), 1)
        == lax.broadcasted_iota(jnp.int32, (k_local, k_whole), 0) + row * k_local,
        1.0,
        0.0,
    ).astype(jnp.bfloat16)
    own_grad_c, own_image_c = nt(chosen, grad_c), nt(chosen, image_c)

    settle(s_all, wide - 1, s_sem.at[1])
    tile = jnp.sum(s_all[...], axis=0)
    norm_0 = tile[:, 0:1] + known_gg
    curve_0 = tile[:, 1:2] + known_gh + damping * norm_0
    image_2 = tile[:, 2:3] + known_qq
    image_3 = tile[:, 3:4] + known_qh + damping * image_2

    alpha_0 = norm_0 / curve_0
    norm_1 = norm_0 - 2.0 * alpha_0 * curve_0 + alpha_0 * alpha_0 * image_2
    beta = norm_1 / norm_0
    gain = 1.0 + beta
    curve_1 = gain * gain * curve_0 - 2.0 * gain * alpha_0 * image_2 + alpha_0 * alpha_0 * image_3
    alpha_1 = norm_1 / curve_1
    on_grad = alpha_0 + alpha_1 * gain
    on_image = -alpha_1 * alpha_0
    out_a[...] = on_grad * grad_a + on_image * image_a
    out_b[...] = on_grad * grad_b + on_image * image_b
    out_c[...] = on_grad * own_grad_c + on_image * own_image_c
    stores = [
        pltpu.make_async_copy(src, dst, out_sem.at[at])
        for at, (src, dst) in enumerate(((out_a, a_out), (out_b, b_out), (out_c, c_out)))
    ]
    for store in stores:
        store.start()

    settle(c_all, narrow - 1, c_sem.at[0])
    settle(b_all.at[0], chips - 1, b_sem.at[0])
    settle(b_all.at[0], chips, cross_sem.at[0])
    settle(pb_half, chips, half_sem.at[0])
    settle(pb_all, chips - 1, pb_sem.at[0])
    settle(p_all, group - 1, p_sem.at[0])
    settle(w_all, high - 1, w_sem.at[0])
    settle(m_all, narrow - 1, m_sem.at[0])
    settle(s_all, wide - 1, s_sem.at[0])
    for store in stores:
        store.wait()


def write_out(in_a, in_b, in_c, out_a, out_b, out_c, held_a, held_b, held_c, sems):
    held = (held_a, held_b, held_c)
    for at, pairs in enumerate((zip((in_a, in_b, in_c), held), zip(held, (out_a, out_b, out_c)))):
        copies = [
            pltpu.make_async_copy(src, dst, sems.at[at, to]) for to, (src, dst) in enumerate(pairs)
        ]
        for copy in copies:
            copy.start()
        for copy in copies:
            copy.wait()


def on_device(wide, narrow, tensor, factor_a, factor_b, factor_c):
    k_local, i_local, j_whole = tensor.shape
    rank, j_local = factor_b.shape
    flattened = tensor.reshape(k_local * i_local, j_whole)
    anywhere = pl.BlockSpec(memory_space=pltpu.HBM)
    pair = pltpu.SemaphoreType.DMA((2,))
    f32, bf16 = jnp.float32, jnp.bfloat16
    chips = wide // 2
    low = 4 if wide % 4 == 0 else 2
    shapes = (
        jax.ShapeDtypeStruct((rank, i_local), f32),
        jax.ShapeDtypeStruct((rank, j_local), f32),
        jax.ShapeDtypeStruct((k_local, rank), f32),
    )
    held = [pltpu.VMEM(one.shape, f32) for one in shapes]
    steps = pl.pallas_call(
        functools.partial(kernel, wide, narrow, k_local),
        out_shape=shapes,
        in_specs=[anywhere] * 4,
        out_specs=(anywhere,) * 3,
        scratch_shapes=[
            *held,
            pltpu.VMEM((k_local * i_local, j_whole), bf16),
            pltpu.VMEM((rank, i_local), bf16),
            pltpu.VMEM((rank, j_local), bf16),
            pltpu.VMEM((k_local, rank), bf16),
            pltpu.VMEM((narrow, k_local, rank), bf16),
            pltpu.VMEM((2, chips, rank, j_local), bf16),
            pltpu.VMEM((2, chips, rank, j_local), f32),
            pltpu.VMEM((chips, rank, j_local), f32),
            pltpu.VMEM((chips, rank, j_local), f32),
            pltpu.VMEM((low * narrow, rank, 128), bf16),
            pltpu.VMEM((wide // low, rank, 128), bf16),
            pltpu.VMEM((2, rank, 128), f32),
            pltpu.VMEM((narrow, 2, rank, 128), f32),
            pltpu.VMEM((wide, 1, 128), f32),
            pltpu.SemaphoreType.DMA((4,)),
            pltpu.SemaphoreType.DMA((3,)),
            pair, pair, pair, pair, pair, pair, pair, pair, pair,
        ],
        compiler_params=pltpu.CompilerParams(collective_id=0, has_side_effects=True),
    )(flattened, factor_a, factor_b, factor_c.T)
    step_a, step_b, step_c = pl.pallas_call(
        write_out,
        out_shape=shapes,
        in_specs=[anywhere] * 3,
        out_specs=(anywhere,) * 3,
        scratch_shapes=[*held, pltpu.SemaphoreType.DMA((2, 3))],
    )(*steps)
    return step_a, step_b, step_c.T


def solution(mesh):
    placed = (P("narrow", "wide"), P(None, "wide"), P(None, "wide"), P(None, "narrow"))
    return jax.shard_map(
        functools.partial(on_device, mesh.shape["wide"], mesh.shape["narrow"]),
        mesh=mesh,
        in_specs=placed,
        out_specs=(P(None, "wide"), P(None, "wide"), P(None, "narrow")),
        check_vma=False,
    )
```
